32 devices in a mesh: gx: 8 (over z, x), gy: 4 (over y, core).
Axes of the slice: x: 2, y: 2, z: 4, core: 2. Of those that a mesh axis runs over, the one named last changes fastest.
Arguments:
- rhs: float32 [48, 3, 256, 512], P(None, None, 'gx', 'gy'), may hold values from -13 to 13
- stiffness: float32 [2, 256, 512], P(None, 'gx', 'gy'), may hold values from 0.2 to 5
- coupling: float32 [2, 256, 512], P(None, 'gx', 'gy'), may hold values from 0.1 to 2
- edges: float32 [12, 256, 512], P(None, 'gx', 'gy'), may hold values from -4 to 4
- flip: int32 [256, 512], P('gx', 'gy'), may hold values from 0 to 1
- pinned: int32 [256, 512], P('gx', 'gy'), may hold values 0 or 1
Outputs:
- solution: float32 [48, 3, 256, 512], P(None, None, 'gx', 'gy')
- residual: float32 [48, 3, 256, 512], P(None, None, 'gx', 'gy')
The draws below stay inside these ranges and needn't reach their ends.
All inputs are finite; a program needn't handle non-finite values. No bound on the sum of `pinned` on one device may be relied on, other than what follows from the above.
Results may differ from the reference program's by a relative error of at most 0.0003.
Values sent between devices are 32-bit elements; how exact they have to be, the bound alone decides.
No kernel may reach another device: no remote copies, remote signals or barrier semaphores. Data moves between devices by JAX's collectives and lax.ppermute only.
A program may use at most 128 MiB of HBM per device.

```python
import math
import jax
import jax.numpy as jnp
from jax import lax

LOADS = 48
ITERS = 6
NX = 256
NY = 512


def draw_rhs(key, part):
    rows = jnp.arange(NX, dtype=jnp.float32) / max(NX - 1, 1)
    columns = jnp.arange(NY, dtype=jnp.float32) / max(NY - 1, 1)
    scaling = (1.0 + 0.8 * rows)[:, None] * (1.0 + 0.8 * columns)[None, :]
    shape = (LOADS, 3, NX, NY)
    base = jax.random.truncated_normal(key, -4.0, 4.0, shape, jnp.float32)
    return (base * scaling).astype(jnp.float32)


def touch_ends(entries, own_key, low, largest):
    place = [jax.random.randint(jax.random.fold_in(own_key, axis), (), 0, length) for axis, length in enumerate(entries.shape)]
    main_axis = entries.shape.index(max(entries.shape))
    neighbour = place[:main_axis] + [(place[main_axis] + 1) % entries.shape[main_axis]] + place[main_axis + 1:]
    return entries.at[tuple(place)].set(low).at[tuple(neighbour)].set(largest)


def levels(rng, extent, split, low, largest):
    gain = 1.0
    for axis_at, parts in split:
        steps = jax.random.uniform(jax.random.fold_in(jax.random.fold_in(rng, 6), axis_at), (parts,), jnp.float32, low / len(split), largest / len(split))
        gain = gain * jnp.repeat(jnp.exp(steps), extent[axis_at] // parts).reshape((-1,) + (1,) * (len(extent) - 1 - axis_at))
    return gain


def normal_values(rng, extent, width, most, shards=(), kind=jnp.bfloat16):
    factor_of = levels(rng, extent, shards, -0.22, 0.18) if shards else 1.0
    values = jax.random.normal(rng, extent, jnp.float32) * width * factor_of
    return jnp.minimum(jnp.maximum(values, -most), most).astype(kind)


def setup_inputs(seed: int = 0) -> dict:
    streams_of = jax.random.split(jax.random.key(seed), 7)
    rhs = draw_rhs(jax.random.fold_in(streams_of[6], 71), 0)
    stiffness = jnp.clip(jnp.exp(math.log(5.0) - 3.218876 * jax.random.uniform(streams_of[1], (2, NX, NY), jnp.float32) ** levels(streams_of[1], (2, NX, NY), ((1, 8), (2, 4)), -0.2, 0.2)), 0.2, 5.0)
    coupling = jnp.clip(jnp.exp(math.log(2.0) - 2.9957323 * jax.random.uniform(streams_of[2], (2, NX, NY), jnp.float32) ** levels(streams_of[2], (2, NX, NY), ((1, 8), (2, 4)), -0.2, 0.2)), 0.1, 2.0)
    edges = normal_values(streams_of[3], (12, NX, NY), 0.6, 4.0, ((1, 8), (2, 4)), jnp.float32)
    flip = touch_ends(jax.random.randint(streams_of[4], (NX, NY), 0, 2), jax.random.fold_in(streams_of[4], 1), 0, 1).astype(jnp.int32)
    pinned = touch_ends((jax.random.randint(streams_of[5], (NX, NY), 0, 8) < 1).astype(jnp.int32), jax.random.fold_in(streams_of[5], 1), 0, 1)
    return {"rhs": rhs, "stiffness": stiffness, "coupling": coupling, "edges": edges, "flip": flip, "pinned": pinned}


damping = 0.2


def triangle(corner_p, corner_q, corner_r, stiffness, couple, dir_one, dir_two):
    edge_one = corner_q - corner_p
    edge_two = corner_r - corner_p
    stretch = jnp.sum(dir_one * edge_one + dir_two * edge_two, axis=-3, keepdims=True)
    force_one = stiffness * edge_one + couple * stretch * dir_one
    force_two = stiffness * edge_two + couple * stretch * dir_two
    return force_one, force_two


def apply_element_hessian(vertex_extended, parameters):
    first_corner = vertex_extended[..., :-1, :-1]
    second_corner = vertex_extended[..., 1:, :-1]
    third_corner = vertex_extended[..., :-1, 1:]
    fourth_corner = vertex_extended[..., 1:, 1:]
    flipped = parameters[16] > 0.5
    force_one, force_two = triangle(first_corner, second_corner, jnp.where(flipped, fourth_corner, third_corner), parameters[0], parameters[2], parameters[4:7], parameters[7:10])
    other_one, other_two = triangle(jnp.where(flipped, first_corner, fourth_corner), jnp.where(flipped, fourth_corner, third_corner), jnp.where(flipped, third_corner, second_corner), parameters[1], parameters[3], parameters[10:13], parameters[13:16])
    zero_part = jnp.zeros_like(force_one)
    minus_one = -(force_one + force_two)
    minus_two = -(other_one + other_two)
    acc_a = minus_one + jnp.where(flipped, minus_two, zero_part)
    acc_b = force_one + jnp.where(flipped, zero_part, other_two)
    acc_c = jnp.where(flipped, zero_part, force_two) + jnp.where(flipped, other_two, other_one)
    acc_d = jnp.where(flipped, force_two, zero_part) + jnp.where(flipped, other_one, minus_two)
    leading_dims = [(0, 0)] * (vertex_extended.ndim - 2)
    return (jnp.pad(acc_a, leading_dims + [(0, 1), (0, 1)]) + jnp.pad(acc_b, leading_dims + [(1, 0), (0, 1)])
            + jnp.pad(acc_c, leading_dims + [(0, 1), (1, 0)]) + jnp.pad(acc_d, leading_dims + [(1, 0), (1, 0)]))


def hessian(direction, parameters, free, pin_weight):
    masked = free * direction
    padded = jnp.pad(masked, [(0, 0), (0, 0), (0, 1), (0, 1)])
    forces = lax.map(lambda single: apply_element_hessian(single, parameters), padded)[..., :-1, :-1]
    return free * (forces + damping * direction) + pin_weight * direction


def inner(left, right):
    return jnp.sum(left * right, axis=(1, 2, 3))


def expand(values):
    return values[:, None, None, None]


def reference(rhs, stiffness, coupling, edges, flip, pinned):
    parameters = jnp.concatenate([stiffness, coupling, edges, flip.astype(jnp.float32)[None]], axis=0)
    free = (1 - pinned).astype(jnp.float32)
    pin_weight = pinned.astype(jnp.float32)
    solution = jnp.zeros_like(rhs)
    residual = rhs
    direction = rhs
    norm_now = inner(residual, residual)
    for iteration in range(ITERS):
        image = hessian(direction, parameters, free, pin_weight)
        alpha = norm_now / inner(direction, image)
        solution = solution + expand(alpha) * direction
        residual = residual - expand(alpha) * image
        norm_next = inner(residual, residual)
        direction = residual + expand(norm_next / norm_now) * direction
        norm_now = norm_next
    return solution, residual
```

```python
import functools
import jax
import jax.numpy as jnp
from jax import lax
from jax.experimental import pallas as pl
from jax.experimental.pallas import tpu as pltpu
from jax.sharding import PartitionSpec as P

DAMP = 0.2
HALO = 6
TOP = 12
PITCH = 32
PER = 4
NCOEF = 20
F32 = jnp.float32


def two_sum(a, b):
    s = a + b
    t = s - a
    return s, (a - (s - t)) + (b - t)


def quick(a, b):
    s = a + b
    return s, b - (s - a)


def halves(a):
    t = 4097.0 * a
    high = t - (t - a)
    return high, a - high


def two_mul(a, b):
    p = a * b
    ah, al = halves(a)
    bh, bl = halves(b)
    return p, ((ah * bh - p) + ah * bl + al * bh) + al * bl


def dd_add(x, y):
    s, e = two_sum(x[0], y[0])
    return quick(s, e + (x[1] + y[1]))


def dd_neg(x):
    return -x[0], -x[1]


def dd_sub(x, y):
    return dd_add(x, dd_neg(y))


def dd_mul(x, y):
    p, e = two_mul(x[0], y[0])
    return quick(p, e + (x[0] * y[1] + x[1] * y[0]))


def dd_div(x, y):
    q = x[0] / y[0]
    p, e = two_mul(q, y[0])
    rest = ((x[0] - p) - e) + (x[1] - q * y[1])
    return quick(q, rest / y[0])


def lift(x):
    return x, jnp.zeros_like(x)


def dd_fma(x, a, y):
    return dd_sub(x, dd_mul(a, y))


def first_block(m):
    one = [dd_div(m[1], m[0])]
    a0 = one[0]
    s1 = {l: dd_fma(m[l + 1], a0, m[l]) for l in range(1, 5)}
    q1 = dd_div(s1[2], s1[1])
    a1 = dd_sub(q1, a0)
    b1 = dd_div(s1[1], m[0])
    s2 = {l: dd_fma(dd_fma(s1[l + 1], a1, s1[l]), b1, m[l]) for l in range(2, 4)}
    a2 = dd_sub(dd_div(s2[3], s2[2]), q1)
    b2 = dd_div(s2[2], s1[1])
    return (a0, a1, a2), (b1, b2), s2[2]


def second_block(nu, a, b, b3):
    a0, a1, a2 = a
    b1, b2 = b
    t2 = {1: nu[0]}
    t2[2] = dd_add(nu[1], dd_mul(a2, t2[1]))
    t12 = nu[0]
    t2[3] = dd_add(dd_add(nu[2], dd_mul(a2, t2[2])), dd_mul(b2, t12))
    t13 = dd_add(t2[2], dd_mul(a1, t12))
    t2[4] = dd_add(dd_add(nu[3], dd_mul(a2, t2[3])), dd_mul(b2, t13))
    a3 = dd_div(nu[1], nu[0])
    t4 = {j: dd_fma(dd_fma(nu[j + 1], a3, nu[j]), b3, t2[j]) for j in range(1, 5)}
    b4 = dd_div(t4[1], nu[0])
    q4 = dd_div(t4[2], t4[1])
    a4 = dd_sub(q4, a3)
    t5 = {j: dd_fma(dd_fma(t4[j + 1], a4, t4[j]), b4, nu[j]) for j in (2, 3)}
    b5 = dd_div(t5[2], t4[1])
    a5 = dd_sub(dd_div(t5[3], t5[2]), q4)
    return (a3, a4, a5), (b4, b5)


def steps_of(a, b, before):
    alphas, sigmas = [], []
    for ak, bk in zip(a, b):
        if before is None:
            alpha = 1.0 / (ak + DAMP)
            sigma = jnp.zeros_like(alpha)
        else:
            ratio = bk * before
            alpha = 1.0 / (ak + DAMP - ratio)
            sigma = alpha * ratio
        alphas.append(alpha)
        sigmas.append(sigma)
        before = alpha
    return alphas, sigmas


def early_residuals(alphas, sigmas):
    one = jnp.ones_like(alphas[0])
    zero = jnp.zeros_like(one)
    polys = [[one, zero, zero, zero]]
    pins = [one]
    for k in range(3):
        now = polys[-1]
        old = polys[-2] if k else [zero] * 4
        lead = 1.0 + sigmas[k] - DAMP * alphas[k]
        polys.append([
            lead * now[i] - (alphas[k] * now[i - 1] if i else zero) - sigmas[k] * old[i]
            for i in range(4)
        ])
        pins.append((1.0 + sigmas[k] - alphas[k]) * pins[-1] - (sigmas[k] * pins[-2] if k else zero))
    return polys, pins


PIN = 1.0 - DAMP


def with_pins(sums, weight):
    out = []
    factor = 1.0
    for k in range(6):
        out.append(dd_add(lift(sums[k]), dd_mul(lift(weight), lift(jnp.full_like(weight, factor)))))
        factor *= PIN
    return out


def row(ref, i):
    return ref[i:i + 1, :]


def middle_scalars(sums_ref, keep_ref):
    sums = [row(sums_ref, i) for i in range(7)]
    m = with_pins(sums, sums[6])
    a, b, top = first_block(m)
    alphas, sigmas = steps_of([x[0] for x in a], [None] + [x[0] for x in b], None)
    polys, pins = early_residuals(alphas, sigmas)
    lead = alphas[0] * alphas[1] * alphas[2]
    values = list(polys[3]) + [pins[3], pins[2]]
    values += [x for pair in a + b for x in pair]
    values += [top[0], sums[6]] + alphas + sigmas + [lead]
    for i, value in enumerate(values):
        keep_ref[i:i + 1, :] = value


def last_scalars(keep_ref, sums_ref, out_ref):
    kept = [row(keep_ref, i) for i in range(25)]
    pins = [kept[5], kept[4]]
    a = [(kept[6 + 2 * i], kept[7 + 2 * i]) for i in range(3)]
    b = [(kept[12 + 2 * i], kept[13 + 2 * i]) for i in range(2)]
    top, weight = kept[16], kept[17]
    alphas, sigmas = kept[18:21], kept[21:24]
    lead = kept[24]
    nu = with_pins([row(sums_ref, i) for i in range(6)], weight * kept[4] * kept[4])
    b3 = dd_div(nu[0], dd_mul(lift(top), dd_mul(lift(lead), lift(lead))))
    a_late, b_late = second_block(nu, a, b, b3)
    more, more_sigmas = steps_of(
        [x[0] for x in a_late], [b3[0]] + [x[0] for x in b_late], alphas[2]
    )
    alphas = alphas + more
    sigmas = sigmas + more_sigmas
    one = jnp.ones_like(top)
    zero = jnp.zeros_like(top)

    def unit(i):
        return [one if j == i else zero for j in range(7)]

    def scale(f, v):
        return [f * x for x in v]

    def plus(*vs):
        total = list(vs[0])
        for v in vs[1:]:
            total = [p + q for p, q in zip(total, v)]
        return total

    residuals = [unit(0), unit(1), unit(2), unit(3)]

    def times_h(v):
        out = [zero] * 7
        for k in range(3):
            image = scale((1.0 + sigmas[k]) / alphas[k] - DAMP, unit(k))
            image[k + 1] = image[k + 1] - 1.0 / alphas[k]
            if k:
                image[k - 1] = image[k - 1] - sigmas[k] / alphas[k]
            out = plus(out, scale(v[k], image))
        for k in range(3, 6):
            out[k + 1] = out[k + 1] + v[k]
        return out

    for k in range(3, 6):
        now, old = residuals[k], residuals[k - 1]
        residuals.append(plus(
            scale(1.0 + sigmas[k] - DAMP * alphas[k], now),
            scale(-alphas[k], times_h(now)),
            scale(-sigmas[k], old),
        ))
        pins.append((1.0 + sigmas[k] - alphas[k]) * pins[-1] - sigmas[k] * pins[-2])
    answers = [[zero] * 7, scale(alphas[0], unit(0))]
    for k in range(1, 6):
        answers.append(plus(
            scale(1.0 + sigmas[k], answers[k]), scale(alphas[k], residuals[k]), scale(-sigmas[k], answers[k - 1])
        ))
    polys, early = early_residuals(alphas[:3], sigmas[:3])
    pins_all = early[:3] + pins[1:]
    pin_answers = [zero, alphas[0]]
    for k in range(1, 6):
        pin_answers.append(
            (1.0 + sigmas[k]) * pin_answers[k] + alphas[k] * pins_all[k] - sigmas[k] * pin_answers[k - 1]
        )
    rows = []
    for v, pin in ((answers[6], pin_answers[6]), (residuals[6], pins_all[6])):
        for i in range(3):
            rows.append(v[0] * polys[0][i] + v[1] * polys[1][i] + v[2] * polys[2][i])
        rows += v[3:] + [pin]
    for i, value in enumerate(rows):
        out_ref[i:i + 1, :] = value


def lanes(rows=8):
    return lax.broadcasted_iota(jnp.int32, (rows, 128), 1)


def prepare_kernel(raw_ref, strip_ref, main_out, strip_out):
    height = raw_ref.shape[2]
    lane = lax.broadcasted_iota(jnp.int32, (height, 128), 1)
    line = lax.broadcasted_iota(jnp.int32, (height, 128), 0)
    near = None
    for which, (src, dst) in enumerate(((strip_ref, strip_out), (raw_ref, main_out))):
        def raw(i):
            return src[i // 3, i % 3]
        flipped = raw(16) > 0.5
        zero = jnp.zeros((height, 128), F32)
        k1, k2 = raw(0), raw(1)
        root1, root2 = jnp.sqrt(raw(2)), jnp.sqrt(raw(3))
        other = jnp.where(flipped, zero, k2)
        left = pltpu.roll(other, 1, 1)
        if which == 1:
            left = jnp.where(lane == 0, near, left)
        else:
            near = pltpu.roll(other, 128 - (HALO - 1), 1)
        below = jnp.where(line == 0, zero, pltpu.roll(other, 1, 0))
        dst[0] = k1 + left
        dst[1] = jnp.where(flipped, k2, k1) + below
        dst[2] = jnp.where(flipped, k1 + k2, zero)
        for c in range(3):
            dst[3 + c] = root1 * raw(4 + c)
            dst[6 + c] = root1 * raw(7 + c)
            one = root2 * raw(10 + c)
            two = root2 * raw(13 + c)
            dst[9 + c] = jnp.where(flipped, zero, two)
            dst[12 + c] = jnp.where(flipped, two, one)
            dst[15 + c] = jnp.where(flipped, one, -(one + two))
        dst[18] = raw(16)
        dst[19] = raw(17)


def dot3(p, q):
    return p[0] * q[0] + p[1] * q[1] + p[2] * q[2]


def tile_step(get, coef, beside, spill, put, put_spill, scratch, first, chunks):
    side, down_b, down_d = scratch
    stop = first + 8 * chunks
    for r in list(range(first, stop, 8)) + [stop - 7]:
        for c in range(3):
            side[c, r:r + 8, :] = beside(c, r, get(c, r))
    for r in range(first, stop, 8):
        def co(i):
            return coef[i, r:r + 8, :]
        flipped = co(18) > 0.5
        base = [get(c, r) for c in range(3)]
        eb = [get(c, r + 1) - base[c] for c in range(3)]
        ec = [side[c, r:r + 8, :] - base[c] for c in range(3)]
        ed = [side[c, r + 1:r + 9, :] - base[c] for c in range(3)]
        ex = [jnp.where(flipped, ed[c], ec[c]) for c in range(3)]
        g1 = [co(3 + c) for c in range(3)]
        g2 = [co(6 + c) for c in range(3)]
        hb = [co(9 + c) for c in range(3)]
        hc = [co(12 + c) for c in range(3)]
        hd = [co(15 + c) for c in range(3)]
        s1 = dot3(g1, eb) + dot3(g2, ex)
        s2 = dot3(hb, eb) + dot3(hc, ec) + dot3(hd, ed)
        zero = jnp.zeros_like(s1)
        s1c = jnp.where(flipped, zero, s1)
        s1d = jnp.where(flipped, s1, zero)
        wv, wh, wd, free = co(0), co(1), co(2), co(19)
        for c in range(3):
            fb = wv * eb[c] + s1 * g1[c] + s2 * hb[c]
            fc = wh * ec[c] + s1c * g2[c] + s2 * hc[c]
            fd = wd * ed[c] + s1d * g2[c] + s2 * hd[c]
            down_b[c, r:r + 8, :] = fb
            down_d[c, r:r + 8, :] = fd
            own = down_b[c, r - 1:r + 7, :] - (fb + fc + fd)
            q = fc + down_d[c, r - 1:r + 7, :]
            if put_spill is not None:
                put_spill(c, r, q)
            put(c, r, free * (own + spill(c, r, q)))


def apply_group(src_main, src_strip, dst_main, dst_strip, coef_main, coef_strip, scratch, first, chunks):
    side, down_b, down_d, strip_q = scratch
    buffers = (side, down_b, down_d)
    lane = lanes()

    def put_strip(c, r, x):
        if dst_strip is not None:
            dst_strip[c, r:r + 8, :] = x

    def put_q(c, r, x):
        strip_q[c, r:r + 8, :] = x

    tile_step(
        lambda c, r: src_strip[c, r:r + 8, :],
        coef_strip,
        lambda c, r, x: pltpu.roll(x, 127, 1),
        lambda c, r, x: pltpu.roll(x, 1, 1),
        put_strip,
        put_q,
        buffers, first, chunks,
    )

    def one(i, carry):
        base = 3 * i
        to_last = (127 - (PITCH * i + 21)) % 128
        to_first = (128 - (PITCH * i + HALO - 1)) % 128

        def beside(c, r, x):
            beyond = pltpu.roll(src_strip[c, r:r + 8, :], to_last, 1)
            return jnp.where(lane == 127, beyond, pltpu.roll(x, 127, 1))

        def spill(c, r, x):
            beyond = pltpu.roll(strip_q[c, r:r + 8, :], to_first, 1)
            return jnp.where(lane == 0, beyond, pltpu.roll(x, 1, 1))

        def put(c, r, x):
            dst_main[base + c, r:r + 8, :] = x

        tile_step(
            lambda c, r: src_main[base + c, r:r + 8, :],
            coef_main, beside, spill, put, None, buffers, first, chunks,
        )
        return carry

    for i in range(PER):
        one(i, 0)


def fold(x):
    return jnp.sum(x, axis=0, keepdims=True)


def inner(p_ref, q_ref, i, p_at, q_at, height):
    total = None
    for c in range(3):
        for r in range(0, height, 8):
            t = p_ref[3 * i + c, p_at + r:p_at + r + 8, :] * q_ref[3 * i + c, q_at + r:q_at + r + 8, :]
            total = t if total is None else total + t
    return fold(total)


def clear(scratch):
    for ref in scratch:
        ref[...] = jnp.zeros(ref.shape, F32)


def first_kernel(height, rhs_ref, u0, s0, cm, cs, u1, u2, u3, s1, s2, s3, sums_ref, side, down_b, down_d, strip_q):
    scratch = (side, down_b, down_d, strip_q)

    @pl.when(pl.program_id(0) == 0)
    def _():
        clear(scratch)

    sv = lambda ref: ref.at[0]
    apply_group(u0, sv(s0), u1, sv(s1), cm, cs, scratch, TOP - 6, (height + 16) // 8)
    apply_group(u1, sv(s1), u2, sv(s2), cm, cs, scratch, TOP - 5, (height + 16) // 8)
    apply_group(u2, sv(s2), u3, sv(s3), cm, cs, scratch, TOP - 4, (height + 8) // 8)
    chain = (u0, u1, u2, u3)
    for i in range(PER):
        rows = []
        for k in range(6):
            rows.append(inner(chain[k // 2], chain[(k + 1) // 2], i, TOP, TOP, height))
        total = None
        for c in range(3):
            for r in range(0, height, 8):
                t = rhs_ref[3 * i + c, r:r + 8, :] - u0[3 * i + c, TOP + r:TOP + r + 8, :]
                t = t * t
                total = t if total is None else total + t
        rows.append(fold(total))
        rows.append(jnp.zeros((1, 128), F32))
        for k in range(8):
            sums_ref[8 * i + k:8 * i + k + 1, :] = rows[k]


def spread(table, load, i):
    return jnp.broadcast_to(table[pl.ds(load, 1), i:i + 1], (8, 128))


def transposed(keep, square, table):
    square[...] = jnp.zeros((128, 128), F32)
    square[0:32, :] = keep[...]
    table[...] = square[...].T


def second_kernel(height, totals_ref, u0, u1, u2, u3, s0, s1, s2, s3, cm, cs,
                  o0, o1, o2, o3, sums_ref, keep_ref, side, down_b, down_d, strip_q,
                  square, table, w0, w1, w2, w3, t0, t1, t2):
    scratch = (side, down_b, down_d, strip_q)
    group = pl.program_id(0)

    @pl.when(group == 0)
    def _():
        clear(scratch)
        clear((w0, w1, w2, w3, t0, t1, t2))
        keep_ref[...] = jnp.zeros(keep_ref.shape, F32)
        middle_scalars(totals_ref, keep_ref)
        transposed(keep_ref, square, table)

    chunks = (height + 8) // 8
    window = range(TOP - 4, TOP - 4 + 8 * chunks, 8)
    segment = lanes() // PITCH
    weights = [[spread(table, group * PER + i, j) for j in range(4)] for i in range(PER)]
    for i in range(PER):
        for c in range(3):
            for r in window:
                w0[3 * i + c, r:r + 8, :] = (
                    weights[i][0] * u0[3 * i + c, r:r + 8, :] + weights[i][1] * u1[3 * i + c, r:r + 8, :]
                    + weights[i][2] * u2[3 * i + c, r:r + 8, :] + weights[i][3] * u3[3 * i + c, r:r + 8, :]
                )
    mixed = []
    for j in range(4):
        m = weights[0][j]
        for i in range(1, PER):
            m = jnp.where(segment == i, weights[i][j], m)
        mixed.append(m)
    for c in range(3):
        for r in window:
            t0[c, r:r + 8, :] = (
                mixed[0] * s0[0, c, r:r + 8, :] + mixed[1] * s1[0, c, r:r + 8, :]
                + mixed[2] * s2[0, c, r:r + 8, :] + mixed[3] * s3[0, c, r:r + 8, :]
            )
    apply_group(w0, t0, w1, t1, cm, cs, scratch, TOP - 4, chunks)
    apply_group(w1, t1, w2, t2, cm, cs, scratch, TOP - 4, chunks)
    apply_group(w2, t2, w3, None, cm, cs, scratch, TOP - 4, chunks)
    chain = (w0, w1, w2, w3)
    for i in range(PER):
        for k in range(6):
            sums_ref[8 * i + k:8 * i + k + 1, :] = inner(chain[k // 2], chain[(k + 1) // 2], i, TOP, TOP, height)
        sums_ref[8 * i + 6:8 * i + 8, :] = jnp.zeros((2, 128), F32)
        for src, dst in zip(chain, (o0, o1, o2, o3)):
            for c in range(3):
                dst[3 * i + c, :, :] = src[3 * i + c, TOP:TOP + height, :]


def last_kernel(height, totals_ref, keep_ref, rhs_ref, u0, u1, u2, w0, w1, w2, w3, x_ref, r_ref, rows, square, table):
    group = pl.program_id(0)

    @pl.when(group == 0)
    def _():
        rows[...] = jnp.zeros(rows.shape, F32)
        last_scalars(keep_ref, totals_ref, rows)
        transposed(rows, square, table)

    for i in range(PER):
        f = [spread(table, group * PER + i, j) for j in range(16)]
        for c in range(3):
            k = 3 * i + c
            for r in range(0, height, 8):
                own = [ref[k, TOP + r:TOP + r + 8, :] for ref in (u0, u1, u2)]
                late = [ref[k, r:r + 8, :] for ref in (w0, w1, w2, w3)]
                pin = rhs_ref[k, r:r + 8, :] - own[0]
                vectors = own + late + [pin]
                for out, at in ((x_ref, 0), (r_ref, 8)):
                    total = f[at] * vectors[0]
                    for j in range(1, 8):
                        total = total + f[at + j] * vectors[j]
                    out[k, r:r + 8, :] = total


def pack_kernel(height, ext, data_ref, up_ref, down_ref, free_ref, u_ref, own_ref, right_ref, left_ref):
    q = pl.program_id(1)
    lane = lanes() % PITCH
    segment = lanes() // PITCH

    @pl.when(q == 0)
    def _():
        right_ref[...] = jnp.zeros(right_ref.shape, F32)
        left_ref[...] = jnp.zeros(left_ref.shape, F32)

    own_ref[...] = jnp.zeros(own_ref.shape, F32)
    for i in range(PER):
        for c in range(3):
            k = 3 * i + c
            u_ref[k, 0:8, :] = jnp.zeros((8, 128), F32)
            u_ref[k, ext - 8:ext, :] = jnp.zeros((8, 128), F32)
            u_ref[k, TOP:TOP + height, :] = data_ref[k, :, :]
            u_ref[k, TOP - HALO:TOP, :] = down_ref[k * HALO:(k + 1) * HALO, :]
            u_ref[k, TOP + height:TOP + height + HALO, :] = up_ref[k * HALO:(k + 1) * HALO, :]
            for r in range(0, ext, 8):
                x = u_ref[k, r:r + 8, :] * free_ref[0, r:r + 8, :]
                u_ref[k, r:r + 8, :] = x
                here = segment == i
                own = own_ref[0, c, r:r + 8, :]
                own = jnp.where(here & (lane >= 6) & (lane < 12), pltpu.roll(x, PITCH * i + 6, 1), own)
                own = jnp.where(here & (lane >= 16) & (lane < 21), pltpu.roll(x, (PITCH * i + 16 - 123) % 128, 1), own)
                own_ref[0, c, r:r + 8, :] = own
                spot = here & (lane >= 8 * q) & (lane < 8 * q + HALO)
                right_ref[0, c, r:r + 8, :] = jnp.where(
                    spot, pltpu.roll(x, (PITCH * i + 8 * q + HALO) % 128, 1), right_ref[0, c, r:r + 8, :])
                left_ref[0, c, r:r + 8, :] = jnp.where(
                    spot, pltpu.roll(x, (PITCH * i + 8 * q) % 128, 1), left_ref[0, c, r:r + 8, :])


def join_kernel(ext, own_ref, from_left_ref, from_right_ref, s_ref):
    q = pl.program_id(0) % 4
    lane = lanes() % PITCH
    for c in range(3):
        for r in range(0, ext, 8):
            x = own_ref[0, c, r:r + 8, :]
            x = jnp.where(lane < HALO, pltpu.roll(from_left_ref[0, c, r:r + 8, :], (128 - 8 * q) % 128, 1), x)
            x = jnp.where(
                (lane >= 21) & (lane < 21 + HALO),
                pltpu.roll(from_right_ref[0, c, r:r + 8, :], (128 + 21 - 8 * q) % 128, 1), x)
            s_ref[0, c, r:r + 8, :] = x


def moved(block, axis, distance):
    n = lax.axis_size(axis)
    return lax.ppermute(block, axis, [(i, i + distance) for i in range(n) if 0 <= i + distance < n])


def summed(x):
    for axis in ("gy", "gx"):
        n = lax.axis_size(axis)
        d = 1
        while d < n:
            x = x + lax.ppermute(x, axis, [(i, i ^ d) for i in range(n)])
            d *= 2
    return x


def totals_of(sums, loads):
    return summed(jnp.pad(jnp.sum(sums.reshape(loads, 8, 128), axis=-1).T, [(0, 0), (0, 128 - loads)]))


def params(limit=48):
    return pltpu.CompilerParams(vmem_limit_bytes=limit * 2**20)


def shape(*dims):
    return jax.ShapeDtypeStruct(dims, F32)


def body(rhs, stiffness, coupling, edges, flip, pinned):
    loads, _, height, width = rhs.shape
    ext = height + 24
    groups = loads // PER
    free = (1 - pinned).astype(F32)[None]
    raw = jnp.concatenate([stiffness, coupling, edges, flip.astype(F32)[None], free], axis=0)
    raw = raw.reshape(6, 3, height, width)
    main = rhs.reshape(loads * 3, height, width)
    both = jnp.concatenate([rhs, raw], axis=0)
    count = (loads + 6) * 3
    up = moved(both[:, :, :HALO, :].reshape(count * HALO, width), "gx", -1)
    down = moved(both[:, :, height - HALO:, :].reshape(count * HALO, width), "gx", 1)
    cut = loads * 3 * HALO

    def rows_of_params(x):
        x = x[cut:].reshape(6, 1, 3, HALO, width)
        return jnp.broadcast_to(x, (6, PER, 3, HALO, width)).reshape(-1, width)

    free_ext = jnp.concatenate([
        jnp.zeros((TOP - HALO, width), F32), down[-HALO:], raw[5, 2], up[-HALO:], jnp.zeros((TOP - HALO, width), F32)
    ], axis=0)
    ones = jnp.ones((ext, width), F32)
    masks = jnp.stack([free_ext, ones])
    raw_wide = jnp.broadcast_to(raw[:, None], (6, PER, 3, height, width)).reshape(6 * PER * 3, height, width)

    def pack(data, up_rows, down_rows, mask):
        n = data.shape[0] // (3 * PER)
        merged = (n + 3) // 4
        last = n - 1
        return pl.pallas_call(
            functools.partial(pack_kernel, height, ext),
            grid=(merged, 4),
            in_specs=[
                pl.BlockSpec((3 * PER, height, width), lambda h, q: (jnp.minimum(4 * h + q, last), 0, 0)),
                pl.BlockSpec((3 * PER * HALO, width), lambda h, q: (jnp.minimum(4 * h + q, last), 0)),
                pl.BlockSpec((3 * PER * HALO, width), lambda h, q: (jnp.minimum(4 * h + q, last), 0)),
                pl.BlockSpec((1, ext, width), lambda h, q: (0, 0, 0)),
            ],
            out_specs=[
                pl.BlockSpec((3 * PER, ext, width), lambda h, q: (jnp.minimum(4 * h + q, last), 0, 0)),
                pl.BlockSpec((1, 3, ext, width), lambda h, q: (jnp.minimum(4 * h + q, last), 0, 0, 0)),
                pl.BlockSpec((1, 3, ext, width), lambda h, q: (h, 0, 0, 0)),
                pl.BlockSpec((1, 3, ext, width), lambda h, q: (h, 0, 0, 0)),
            ],
            out_shape=[
                shape(n * 3 * PER, ext, width), shape(n, 3, ext, width),
                shape(merged, 3, ext, width), shape(merged, 3, ext, width),
            ],
            compiler_params=params(),
        )(data, up_rows, down_rows, mask)

    u0, own, to_right, to_left = pack(main, up[:cut], down[:cut], masks[:1])
    p0, p_own, p_right, p_left = pack(raw_wide, rows_of_params(up), rows_of_params(down), masks[1:])
    m = to_right.shape[0]
    all_left = moved(jnp.concatenate([to_right, p_right]), "gy", 1)
    all_right = moved(jnp.concatenate([to_left, p_left]), "gy", -1)

    def join(own_part, from_left, from_right):
        n = own_part.shape[0]
        block = pl.BlockSpec((1, 3, ext, width), lambda g: (g, 0, 0, 0))
        quarter = pl.BlockSpec((1, 3, ext, width), lambda g: (g // 4, 0, 0, 0))
        return pl.pallas_call(
            functools.partial(join_kernel, ext),
            grid=(n,),
            in_specs=[block, quarter, quarter],
            out_specs=block,
            out_shape=shape(n, 3, ext, width),
            compiler_params=params(),
        )(own_part, from_left, from_right)

    s0 = join(own, all_left[:m], all_right[:m])
    p_strip = join(p_own, all_left[m:], all_right[m:])
    p_main = p0.reshape(6, PER, 3, ext, width)[:, 0]
    cm, cs = pl.pallas_call(
        prepare_kernel,
        out_shape=[shape(NCOEF, ext, width), shape(NCOEF, ext, width)],
        compiler_params=params(),
    )(p_main, p_strip)

    tile = pl.BlockSpec((3 * PER, ext, width), lambda g: (g, 0, 0))
    own_tile = pl.BlockSpec((3 * PER, height, width), lambda g: (g, 0, 0))
    strip = pl.BlockSpec((1, 3, ext, width), lambda g: (g, 0, 0, 0))
    table = pl.BlockSpec((NCOEF, ext, width), lambda g: (0, 0, 0))
    part = pl.BlockSpec((8 * PER, width), lambda g: (g, 0))
    tile_shape = shape(loads * 3, ext, width)
    own_shape = shape(loads * 3, height, width)
    strip_shape = shape(groups, 3, ext, width)
    sums_shape = shape(8 * loads, width)
    small = [pltpu.VMEM((3, ext, width), F32)] * 4
    u1, u2, u3, s1, s2, s3, sums = pl.pallas_call(
        functools.partial(first_kernel, height),
        grid=(groups,),
        in_specs=[own_tile, tile, strip, table, table],
        out_specs=[tile] * 3 + [strip] * 3 + [part],
        out_shape=[tile_shape] * 3 + [strip_shape] * 3 + [sums_shape],
        scratch_shapes=small,
        compiler_params=params(),
    )(main, u0, s0, cm, cs)
    totals = totals_of(sums, loads)
    fixed = pl.BlockSpec((8, 128), lambda g: (0, 0))
    kept = pl.BlockSpec((32, 128), lambda g: (0, 0))
    w0, w1, w2, w3, sums, keep = pl.pallas_call(
        functools.partial(second_kernel, height),
        grid=(groups,),
        in_specs=[fixed] + [tile] * 4 + [strip] * 4 + [table] * 2,
        out_specs=[own_tile] * 4 + [part, kept],
        out_shape=[own_shape] * 4 + [sums_shape, shape(32, 128)],
        scratch_shapes=small + [pltpu.VMEM((128, 128), F32)] * 2
        + [pltpu.VMEM((3 * PER, ext, width), F32)] * 4 + [pltpu.VMEM((3, ext, width), F32)] * 3,
        compiler_params=params(),
    )(totals, u0, u1, u2, u3, s0, s1, s2, s3, cm, cs)
    totals = totals_of(sums, loads)
    x, r = pl.pallas_call(
        functools.partial(last_kernel, height),
        grid=(groups,),
        in_specs=[fixed, kept, own_tile] + [tile] * 3 + [own_tile] * 4,
        out_specs=[own_tile] * 2,
        out_shape=[own_shape] * 2,
        scratch_shapes=[pltpu.VMEM((32, 128), F32), pltpu.VMEM((128, 128), F32), pltpu.VMEM((128, 128), F32)],
        compiler_params=params(),
    )(totals, keep, main, u0, u1, u2, w0, w1, w2, w3)
    return x.reshape(rhs.shape), r.reshape(rhs.shape)


def solution(mesh):
    placed = (
        P(None, None, "gx", "gy"),
        P(None, "gx", "gy"),
        P(None, "gx", "gy"),
        P(None, "gx", "gy"),
        P("gx", "gy"),
        P("gx", "gy"),
    )
    return jax.shard_map(
        body,
        mesh=mesh,
        in_specs=placed,
        out_specs=(P(None, None, "gx", "gy"), P(None, None, "gx", "gy")),
        check_vma=False,
    )
```

```python
import functools
import jax
import jax.numpy as jnp
from jax import lax
from jax.experimental import pallas as pl
from jax.experimental.pallas import tpu as pltpu
from jax.sharding import PartitionSpec as P

DAMP = 0.2
HALO = 6
TOP = 12
PITCH = 32
PER = 4
NCOEF = 20
PAIR = 2
F32 = jnp.float32


def two_sum(a, b):
    s = a + b
    t = s - a
    return s, (a - (s - t)) + (b - t)


def quick(a, b):
    s = a + b
    return s, b - (s - a)


def halves(a):
    t = 4097.0 * a
    high = t - (t - a)
    return high, a - high


def two_mul(a, b):
    p = a * b
    ah, al = halves(a)
    bh, bl = halves(b)
    return p, ((ah * bh - p) + ah * bl + al * bh) + al * bl


def dd_add(x, y):
    s, e = two_sum(x[0], y[0])
    return quick(s, e + (x[1] + y[1]))


def dd_neg(x):
    return -x[0], -x[1]


def dd_sub(x, y):
    return dd_add(x, dd_neg(y))


def dd_mul(x, y):
    p, e = two_mul(x[0], y[0])
    return quick(p, e + (x[0] * y[1] + x[1] * y[0]))


def dd_div(x, y):
    q = x[0] / y[0]
    p, e = two_mul(q, y[0])
    rest = ((x[0] - p) - e) + (x[1] - q * y[1])
    return quick(q, rest / y[0])


def lift(x):
    return x, jnp.zeros_like(x)


def dd_fma(x, a, y):
    return dd_sub(x, dd_mul(a, y))


def first_block(m):
    one = [dd_div(m[1], m[0])]
    a0 = one[0]
    s1 = {l: dd_fma(m[l + 1], a0, m[l]) for l in range(1, 5)}
    q1 = dd_div(s1[2], s1[1])
    a1 = dd_sub(q1, a0)
    b1 = dd_div(s1[1], m[0])
    s2 = {l: dd_fma(dd_fma(s1[l + 1], a1, s1[l]), b1, m[l]) for l in range(2, 4)}
    a2 = dd_sub(dd_div(s2[3], s2[2]), q1)
    b2 = dd_div(s2[2], s1[1])
    return (a0, a1, a2), (b1, b2), s2[2]


def second_block(nu, a, b, b3):
    a0, a1, a2 = a
    b1, b2 = b
    t2 = {1: nu[0]}
    t2[2] = dd_add(nu[1], dd_mul(a2, t2[1]))
    t12 = nu[0]
    t2[3] = dd_add(dd_add(nu[2], dd_mul(a2, t2[2])), dd_mul(b2, t12))
    t13 = dd_add(t2[2], dd_mul(a1, t12))
    t2[4] = dd_add(dd_add(nu[3], dd_mul(a2, t2[3])), dd_mul(b2, t13))
    a3 = dd_div(nu[1], nu[0])
    t4 = {j: dd_fma(dd_fma(nu[j + 1], a3, nu[j]), b3, t2[j]) for j in range(1, 5)}
    b4 = dd_div(t4[1], nu[0])
    q4 = dd_div(t4[2], t4[1])
    a4 = dd_sub(q4, a3)
    t5 = {j: dd_fma(dd_fma(t4[j + 1], a4, t4[j]), b4, nu[j]) for j in (2, 3)}
    b5 = dd_div(t5[2], t4[1])
    a5 = dd_sub(dd_div(t5[3], t5[2]), q4)
    return (a3, a4, a5), (b4, b5)


def steps_of(a, b, before):
    alphas, sigmas = [], []
    for ak, bk in zip(a, b):
        if before is None:
            alpha = 1.0 / (ak + DAMP)
            sigma = jnp.zeros_like(alpha)
        else:
            ratio = bk * before
            alpha = 1.0 / (ak + DAMP - ratio)
            sigma = alpha * ratio
        alphas.append(alpha)
        sigmas.append(sigma)
        before = alpha
    return alphas, sigmas


def early_residuals(alphas, sigmas):
    one = jnp.ones_like(alphas[0])
    zero = jnp.zeros_like(one)
    polys = [[one, zero, zero, zero]]
    pins = [one]
    for k in range(3):
        now = polys[-1]
        old = polys[-2] if k else [zero] * 4
        lead = 1.0 + sigmas[k] - DAMP * alphas[k]
        polys.append([
            lead * now[i] - (alphas[k] * now[i - 1] if i else zero) - sigmas[k] * old[i]
            for i in range(4)
        ])
        pins.append((1.0 + sigmas[k] - alphas[k]) * pins[-1] - (sigmas[k] * pins[-2] if k else zero))
    return polys, pins


PIN = 1.0 - DAMP


def with_pins(sums, weight):
    out = []
    factor = 1.0
    for k in range(6):
        out.append(dd_add(sums[k], dd_mul(weight, lift(jnp.full_like(weight[0], factor)))))
        factor *= PIN
    return out


def row(ref, i):
    return ref[i:i + 1, :]


def middle_scalars(sums_ref, keep_ref):
    sums = [(row(sums_ref, i), row(sums_ref, 8 + i)) for i in range(7)]
    m = with_pins(sums, sums[6])
    a, b, top = first_block(m)
    alphas, sigmas = steps_of([x[0] for x in a], [None] + [x[0] for x in b], None)
    polys, pins = early_residuals(alphas, sigmas)
    lead = alphas[0] * alphas[1] * alphas[2]
    values = list(polys[3]) + [pins[3], pins[2]]
    values += [x for pair in a + b for x in pair]
    values += [top[0], sums[6][0]] + alphas + sigmas + [lead]
    for i, value in enumerate(values):
        keep_ref[i:i + 1, :] = value


def last_scalars(keep_ref, sums_ref, out_ref):
    kept = [row(keep_ref, i) for i in range(25)]
    pins = [kept[5], kept[4]]
    a = [(kept[6 + 2 * i], kept[7 + 2 * i]) for i in range(3)]
    b = [(kept[12 + 2 * i], kept[13 + 2 * i]) for i in range(2)]
    top, weight = kept[16], kept[17]
    alphas, sigmas = kept[18:21], kept[21:24]
    lead = kept[24]
    nu = with_pins([(row(sums_ref, i), row(sums_ref, 8 + i)) for i in range(6)], lift(weight * kept[4] * kept[4]))
    b3 = dd_div(nu[0], dd_mul(lift(top), dd_mul(lift(lead), lift(lead))))
    a_late, b_late = second_block(nu, a, b, b3)
    more, more_sigmas = steps_of(
        [x[0] for x in a_late], [b3[0]] + [x[0] for x in b_late], alphas[2]
    )
    alphas = alphas + more
    sigmas = sigmas + more_sigmas
    one = jnp.ones_like(top)
    zero = jnp.zeros_like(top)

    def unit(i):
        return [one if j == i else zero for j in range(7)]

    def scale(f, v):
        return [f * x for x in v]

    def plus(*vs):
        total = list(vs[0])
        for v in vs[1:]:
            total = [p + q for p, q in zip(total, v)]
        return total

    residuals = [unit(0), unit(1), unit(2), unit(3)]

    def times_h(v):
        out = [zero] * 7
        for k in range(3):
            image = scale((1.0 + sigmas[k]) / alphas[k] - DAMP, unit(k))
            image[k + 1] = image[k + 1] - 1.0 / alphas[k]
            if k:
                image[k - 1] = image[k - 1] - sigmas[k] / alphas[k]
            out = plus(out, scale(v[k], image))
        for k in range(3, 6):
            out[k + 1] = out[k + 1] + v[k]
        return out

    for k in range(3, 6):
        now, old = residuals[k], residuals[k - 1]
        residuals.append(plus(
            scale(1.0 + sigmas[k] - DAMP * alphas[k], now),
            scale(-alphas[k], times_h(now)),
            scale(-sigmas[k], old),
        ))
        pins.append((1.0 + sigmas[k] - alphas[k]) * pins[-1] - sigmas[k] * pins[-2])
    answers = [[zero] * 7, scale(alphas[0], unit(0))]
    for k in range(1, 6):
        answers.append(plus(
            scale(1.0 + sigmas[k], answers[k]), scale(alphas[k], residuals[k]), scale(-sigmas[k], answers[k - 1])
        ))
    polys, early = early_residuals(alphas[:3], sigmas[:3])
    pins_all = early[:3] + pins[1:]
    pin_answers = [zero, alphas[0]]
    for k in range(1, 6):
        pin_answers.append(
            (1.0 + sigmas[k]) * pin_answers[k] + alphas[k] * pins_all[k] - sigmas[k] * pin_answers[k - 1]
        )
    rows = []
    for v, pin in ((answers[6], pin_answers[6]), (residuals[6], pins_all[6])):
        for i in range(3):
            rows.append(v[0] * polys[0][i] + v[1] * polys[1][i] + v[2] * polys[2][i])
        rows += v[3:] + [pin]
    for i, value in enumerate(rows):
        out_ref[i:i + 1, :] = value


def lanes(rows=8):
    return lax.broadcasted_iota(jnp.int32, (rows, 128), 1)


def field(refs, i, rows):
    stiffness, coupling, edges, flip, pinned = refs
    if i < 2:
        return stiffness[i, rows, :]
    if i < 4:
        return coupling[i - 2, rows, :]
    if i < 16:
        return edges[i - 4, rows, :]
    if i == 16:
        return flip[rows, :].astype(F32)
    return (1 - pinned[rows, :]).astype(F32)


def join_rows(dst, lead, own, up, down, height):
    ext = dst.shape[-2]
    dst[lead + (slice(0, 8),)] = jnp.zeros((8, 128), F32)
    dst[lead + (slice(ext - 8, ext),)] = jnp.zeros((8, 128), F32)
    dst[lead + (slice(TOP, TOP + height),)] = own
    dst[lead + (slice(TOP - HALO, TOP),)] = down
    dst[lead + (slice(TOP + height, TOP + height + HALO),)] = up


def own_columns(x, i, kept):
    lane = lanes() % PITCH
    here = lanes() // PITCH == i
    kept = jnp.where(here & (lane >= 6) & (lane < 12), pltpu.roll(x, PITCH * i + 6, 1), kept)
    return jnp.where(here & (lane >= 16) & (lane < 21), pltpu.roll(x, (PITCH * i + 16 - 123) % 128, 1), kept)


def other_columns(left, right, q, kept):
    lane = lanes() % PITCH
    kept = jnp.where(lane < HALO, pltpu.roll(left, (128 - 8 * q) % 128, 1), kept)
    return jnp.where(
        (lane >= 21) & (lane < 21 + HALO), pltpu.roll(right, (128 + 21 - 8 * q) % 128, 1), kept)


def join_sides(sides, column, lead, merged, corners, height):
    for n in range(2):
        join_rows(sides, (n, column), merged[n][lead + (slice(None),)], corners[n][lead + (slice(8, 8 + HALO),)],
                  corners[n][lead + (slice(0, HALO),)], height)


def prepare_kernel(loads, merged, stiffness, coupling, edges, flip, pinned, up_ref, down_ref, left_ref, right_ref, left_ends, right_ends,
                   main_out, strip_out, wide, strip, sides):
    refs = (stiffness, coupling, edges, flip, pinned)
    height = flip.shape[0]
    ext = wide.shape[2]
    for p in range(6):
        for c in range(3):
            k = 3 * (loads + p) + c
            join_rows(wide, (p, c), field(refs, 3 * p + c, slice(0, height)), up_ref[k * HALO:(k + 1) * HALO, :],
                      down_ref[k * HALO:(k + 1) * HALO, :], height)
            join_sides(sides, c, (merged + p // 4, c), (left_ref, right_ref), (left_ends, right_ends), height)
            for r in range(0, ext, 8):
                x = wide[p, c, r:r + 8, :]
                total = jnp.zeros((8, 128), F32)
                for i in range(PER):
                    total = own_columns(x, i, total)
                strip[p, c, r:r + 8, :] = other_columns(
                    sides[0, c, r:r + 8, :], sides[1, c, r:r + 8, :], p % 4, total)
    lane = lax.broadcasted_iota(jnp.int32, (ext, 128), 1)
    line = lax.broadcasted_iota(jnp.int32, (ext, 128), 0)
    near = None
    for which, (src, dst) in enumerate(((strip, strip_out), (wide, main_out))):
        def raw(i):
            return src[i // 3, i % 3]
        flipped = raw(16) > 0.5
        zero = jnp.zeros((ext, 128), F32)
        k1, k2 = raw(0), raw(1)
        root1, root2 = jnp.sqrt(raw(2)), jnp.sqrt(raw(3))
        other = jnp.where(flipped, zero, k2)
        left = pltpu.roll(other, 1, 1)
        if which == 1:
            left = jnp.where(lane == 0, near, left)
        else:
            near = pltpu.roll(other, 128 - (HALO - 1), 1)
        below = jnp.where(line == 0, zero, pltpu.roll(other, 1, 0))
        dst[0] = k1 + left
        dst[1] = jnp.where(flipped, k2, k1) + below
        dst[2] = jnp.where(flipped, k1 + k2, zero)
        for c in range(3):
            dst[3 + c] = root1 * raw(4 + c)
            dst[6 + c] = root1 * raw(7 + c)
            one = root2 * raw(10 + c)
            two = root2 * raw(13 + c)
            dst[9 + c] = jnp.where(flipped, zero, two)
            dst[12 + c] = jnp.where(flipped, two, one)
            dst[15 + c] = jnp.where(flipped, one, -(one + two))
        dst[18] = raw(16)
        dst[19] = raw(17)


def dot3(p, q):
    return p[0] * q[0] + p[1] * q[1] + p[2] * q[2]


def tile_step(tiles, coef, first, chunks):
    stop = first + 8 * chunks
    for r in list(range(first, stop, 8)) + [stop - 7]:
        for side, get, beside, _, _, _ in tiles:
            for c in range(3):
                side[c, r:r + 8, :] = beside(c, r, get(c, r))
    top = lax.broadcasted_iota(jnp.int32, (8, 128), 0) == 0
    before = [None] * len(tiles)
    for r in range(first, stop, 8):
        def co(i):
            return coef[i, r:r + 8, :]
        flipped = co(18) > 0.5
        g1 = [co(3 + c) for c in range(3)]
        g2 = [co(6 + c) for c in range(3)]
        hb = [co(9 + c) for c in range(3)]
        hc = [co(12 + c) for c in range(3)]
        hd = [co(15 + c) for c in range(3)]
        wv, wh, wd, free = co(0), co(1), co(2), co(19)
        forces = []
        for side, get, _, _, _, _ in tiles:
            base = [get(c, r) for c in range(3)]
            eb = [get(c, r + 1) - base[c] for c in range(3)]
            ec = [side[c, r:r + 8, :] - base[c] for c in range(3)]
            ed = [side[c, r + 1:r + 9, :] - base[c] for c in range(3)]
            ex = [jnp.where(flipped, ed[c], ec[c]) for c in range(3)]
            s1 = dot3(g1, eb) + dot3(g2, ex)
            s2 = dot3(hb, eb) + dot3(hc, ec) + dot3(hd, ed)
            zero = jnp.zeros_like(s1)
            s1c = jnp.where(flipped, zero, s1)
            s1d = jnp.where(flipped, s1, zero)
            forces.append([(
                wv * eb[c] + s1 * g1[c] + s2 * hb[c],
                wh * ec[c] + s1c * g2[c] + s2 * hc[c],
                wd * ed[c] + s1d * g2[c] + s2 * hd[c],
            ) for c in range(3)])
        for n, (_, _, _, spill, put, put_spill) in enumerate(tiles):
            rolled = []
            for c in range(3):
                fb, fc, fd = forces[n][c]
                down_b, down_d = pltpu.roll(fb, 1, 0), pltpu.roll(fd, 1, 0)
                rolled.append((down_b, down_d))
                if before[n] is not None:
                    down_b = jnp.where(top, before[n][c][0], down_b)
                    down_d = jnp.where(top, before[n][c][1], down_d)
                own = down_b - (fb + fc + fd)
                q = fc + down_d
                if put_spill is not None:
                    put_spill(c, r, q)
                put(c, r, free * (own + spill(c, r, q)))
            before[n] = rolled


def apply_group(src_main, src_strip, dst_main, dst_strip, coef_main, coef_strip, scratch, first, chunks):
    side, strip_q = scratch
    lane = lanes()

    def put_strip(c, r, x):
        if dst_strip is not None:
            dst_strip[c, r:r + 8, :] = x

    def put_q(c, r, x):
        strip_q[c, r:r + 8, :] = x

    tile_step([(
        side.at[0],
        lambda c, r: src_strip[c, r:r + 8, :],
        lambda c, r, x: pltpu.roll(x, 127, 1),
        lambda c, r, x: pltpu.roll(x, 1, 1),
        put_strip,
        put_q,
    )], coef_strip, first, chunks)

    def tile(i, slot):
        base = 3 * i
        to_last = (127 - (PITCH * i + 21)) % 128
        to_first = (128 - (PITCH * i + HALO - 1)) % 128

        def get(c, r):
            return src_main[base + c, r:r + 8, :]

        def beside(c, r, x):
            beyond = pltpu.roll(src_strip[c, r:r + 8, :], to_last, 1)
            return jnp.where(lane == 127, beyond, pltpu.roll(x, 127, 1))

        def spill(c, r, x):
            beyond = pltpu.roll(strip_q[c, r:r + 8, :], to_first, 1)
            return jnp.where(lane == 0, beyond, pltpu.roll(x, 1, 1))

        def put(c, r, x):
            dst_main[base + c, r:r + 8, :] = x

        return side.at[slot], get, beside, spill, put, None

    for i in range(0, PER, PAIR):
        tile_step([tile(i + n, n) for n in range(PAIR)], coef_main, first, chunks)


def add_up(sums, totals_ref):
    totals_ref[...] = jnp.zeros(totals_ref.shape, F32)
    for k in range(7):
        totals_ref[k:k + 1, :] = jnp.sum(sums[k].T, axis=0, keepdims=True)


def fold(x):
    return jnp.sum(x, axis=0, keepdims=True)


def inner(p_ref, q_ref, i, p_at, q_at, height):
    total = None
    for c in range(3):
        for r in range(0, height, 8):
            t = p_ref[3 * i + c, p_at + r:p_at + r + 8, :] * q_ref[3 * i + c, q_at + r:q_at + r + 8, :]
            total = t if total is None else total + t
    return fold(total)


def clear(scratch):
    for ref in scratch:
        ref[...] = jnp.zeros(ref.shape, F32)


def first_kernel(height, rhs_ref, up_ref, down_ref, left_ref, right_ref, left_ends, right_ends, cm, cs,
                 u0_all, u1_all, u2_all, u3_all, s0_all, s1_all, s2_all, s3_all, totals_out, side, strip_q, sides, sums):
    scratch = (side, strip_q)
    group = pl.program_id(0)
    ext = cm.shape[1]

    @pl.when(group == 0)
    def _():
        clear(scratch)
        clear((sums,))

    mine = pl.ds(group * 3 * PER, 3 * PER)
    u0, u1, u2, u3 = (ref.at[mine] for ref in (u0_all, u1_all, u2_all, u3_all))
    s0, s1, s2, s3 = (ref.at[group] for ref in (s0_all, s1_all, s2_all, s3_all))
    q = group % 4
    for c in range(3):
        join_sides(sides, c, (0, c), (left_ref, right_ref), (left_ends, right_ends), height)
        for i in range(PER):
            k = 3 * i + c
            join_rows(u0, (k,), rhs_ref[k, :, :], up_ref[k * HALO:(k + 1) * HALO, :],
                      down_ref[k * HALO:(k + 1) * HALO, :], height)
        for r in range(0, ext, 8):
            total = jnp.zeros((8, 128), F32)
            for i in range(PER):
                x = u0[3 * i + c, r:r + 8, :] * cm[19, r:r + 8, :]
                u0[3 * i + c, r:r + 8, :] = x
                total = own_columns(x, i, total)
            total = other_columns(sides[0, c, r:r + 8, :], sides[1, c, r:r + 8, :], q, total)
            s0[c, r:r + 8, :] = total * cs[19, r:r + 8, :]
    apply_group(u0, s0, u1, s1, cm, cs, scratch, TOP - 6, (height + 16) // 8)
    apply_group(u1, s1, u2, s2, cm, cs, scratch, TOP - 5, (height + 16) // 8)
    apply_group(u2, s2, u3, s3, cm, cs, scratch, TOP - 4, (height + 8) // 8)
    chain = (u0, u1, u2, u3)
    for i in range(PER):
        rows = []
        for k in range(6):
            rows.append(inner(chain[k // 2], chain[(k + 1) // 2], i, TOP, TOP, height))
        total = None
        for c in range(3):
            for r in range(0, height, 8):
                t = rhs_ref[3 * i + c, r:r + 8, :] - u0[3 * i + c, TOP + r:TOP + r + 8, :]
                t = t * t
                total = t if total is None else total + t
        rows.append(fold(total))
        for k in range(7):
            sums[k, pl.ds(group * PER + i, 1), :] = rows[k]

    @pl.when(group == pl.num_programs(0) - 1)
    def _():
        add_up(sums, totals_out)


def spread(table, load, i):
    return jnp.broadcast_to(table[pl.ds(load, 1), i:i + 1], (8, 128))


def transposed(keep, square, table):
    square[...] = jnp.zeros((128, 128), F32)
    square[0:32, :] = keep[...]
    table[...] = square[...].T


def second_kernel(height, totals_ref, u0_all, u1_all, u2_all, u3_all, s0_all, s1_all, s2_all, s3_all, cm, cs,
                  w0_all, w1_all, w2_all, w3_all, totals_out, keep_ref, side, strip_q, square, table, t0, t1, t2, sums):
    scratch = (side, strip_q)
    group = pl.program_id(0)

    @pl.when(group == 0)
    def _():
        clear(scratch)
        clear((sums,))
        keep_ref[...] = jnp.zeros(keep_ref.shape, F32)
        middle_scalars(totals_ref, keep_ref)
        transposed(keep_ref, square, table)

    mine = pl.ds(group * 3 * PER, 3 * PER)
    u0, u1, u2, u3 = (ref.at[mine] for ref in (u0_all, u1_all, u2_all, u3_all))
    w0, w1, w2, w3 = (ref.at[mine] for ref in (w0_all, w1_all, w2_all, w3_all))
    s0, s1, s2, s3 = (ref.at[group] for ref in (s0_all, s1_all, s2_all, s3_all))
    chunks = (height + 8) // 8
    window = range(TOP - 4, TOP - 4 + 8 * chunks, 8)
    segment = lanes() // PITCH
    weights = [[spread(table, group * PER + i, j) for j in range(4)] for i in range(PER)]
    for i in range(PER):
        for c in range(3):
            for r in window:
                w0[3 * i + c, r:r + 8, :] = (
                    weights[i][0] * u0[3 * i + c, r:r + 8, :] + weights[i][1] * u1[3 * i + c, r:r + 8, :]
                    + weights[i][2] * u2[3 * i + c, r:r + 8, :] + weights[i][3] * u3[3 * i + c, r:r + 8, :]
                )
    mixed = []
    for j in range(4):
        m = weights[0][j]
        for i in range(1, PER):
            m = jnp.where(segment == i, weights[i][j], m)
        mixed.append(m)
    for c in range(3):
        for r in window:
            t0[c, r:r + 8, :] = (
                mixed[0] * s0[c, r:r + 8, :] + mixed[1] * s1[c, r:r + 8, :]
                + mixed[2] * s2[c, r:r + 8, :] + mixed[3] * s3[c, r:r + 8, :]
            )
    apply_group(w0, t0, w1, t1, cm, cs, scratch, TOP - 4, chunks)
    apply_group(w1, t1, w2, t2, cm, cs, scratch, TOP - 4, chunks)
    apply_group(w2, t2, w3, None, cm, cs, scratch, TOP - 4, chunks)
    chain = (w0, w1, w2, w3)
    for i in range(PER):
        for k in range(6):
            sums[k, pl.ds(group * PER + i, 1), :] = inner(chain[k // 2], chain[(k + 1) // 2], i, TOP, TOP, height)

    @pl.when(group == pl.num_programs(0) - 1)
    def _():
        add_up(sums, totals_out)


def last_kernel(height, totals_ref, keep_ref, rhs_ref, u0_all, u1_all, u2_all, w0_all, w1_all, w2_all, w3_all,
                x_ref, r_ref, rows, square, table):
    group = pl.program_id(0)

    @pl.when(group == 0)
    def _():
        rows[...] = jnp.zeros(rows.shape, F32)
        last_scalars(keep_ref, totals_ref, rows)
        transposed(rows, square, table)

    mine = pl.ds(group * 3 * PER, 3 * PER)
    basis = [ref.at[mine] for ref in (u0_all, u1_all, u2_all, w0_all, w1_all, w2_all, w3_all)]
    for i in range(PER):
        f = [spread(table, group * PER + i, j) for j in range(16)]
        for c in range(3):
            k = 3 * i + c
            for r in range(0, height, 8):
                vectors = [ref[k, TOP + r:TOP + r + 8, :] for ref in basis]
                vectors.append(rhs_ref[k, r:r + 8, :] - vectors[0])
                for out, at in ((x_ref, 0), (r_ref, 8)):
                    total = f[at] * vectors[0]
                    for j in range(1, 8):
                        total = total + f[at + j] * vectors[j]
                    out[k, r:r + 8, :] = total


def rows_kernel(*refs):
    low_refs, high_refs, outs = refs[:6], refs[6:12], refs[12:]
    loads = low_refs[0].shape[0]
    for j in range(loads + 18):
        to = slice(j * HALO, (j + 1) * HALO)
        for source, rows, out in ((low_refs, slice(0, HALO), outs[0]), (high_refs, slice(8 - HALO, 8), outs[1])):
            if j < loads:
                out[to, :] = source[0][j, rows, :]
            else:
                out[to, :] = field(source[1:], j - loads, rows)


def cut(get, rows, quarters, right_ref, left_ref):
    lane = lanes() % PITCH
    segment = lanes() // PITCH
    for c in range(3):
        for r in rows:
            right = jnp.zeros((8, 128), F32)
            left = right
            for q in range(quarters):
                for i in range(PER):
                    spot = (segment == i) & (lane >= 8 * q) & (lane < 8 * q + HALO)
                    x = get(q, i, c, r)
                    right = jnp.where(spot, pltpu.roll(x, (PITCH * i + 8 * q + HALO) % 128, 1), right)
                    left = jnp.where(spot, pltpu.roll(x, (PITCH * i + 8 * q) % 128, 1), left)
            right_ref[0, c, r:r + 8, :] = right
            left_ref[0, c, r:r + 8, :] = left


def each_group(merged, load_rows, raw_rows, rows, outs):
    group = pl.program_id(0)

    @pl.when(group < merged)
    def _():
        cut(lambda q, i, c, r: load_rows(3 * (PER * q + i) + c, r), rows, 4, *outs)

    for p in (0, 4):
        @pl.when(group == merged + p // 4)
        def _():
            cut(lambda q, i, c, r: raw_rows(3 * (p + q) + c, r), rows, min(4, 6 - p), *outs)


def columns_kernel(merged, height, data_ref, *refs):
    each_group(
        merged, lambda k, r: data_ref[k, r:r + 8, :], lambda k, r: field(refs[:5], k, slice(r, r + 8)),
        range(0, height, 8), refs[5:],
    )


def ends_kernel(merged, fields, down_ref, up_ref, all_down, all_up, right_ref, left_ref, one):
    one[...] = jnp.zeros(one.shape, F32)

    def load_rows(k, r):
        one[0:HALO, :] = (down_ref, up_ref)[r // 8][k * HALO:(k + 1) * HALO, :]
        return one[...]

    def raw_rows(k, r):
        k = k + fields
        one[0:HALO, :] = (all_down, all_up)[r // 8][k * HALO:(k + 1) * HALO, :]
        return one[...]

    each_group(merged, load_rows, raw_rows, (0, 8), (right_ref, left_ref))


def moved(block, axis, distance):
    n = lax.axis_size(axis)
    return lax.ppermute(block, axis, [(i, i + distance) for i in range(n) if 0 <= i + distance < n])


def summed(x):
    half = x.shape[0] // 2
    for axis in ("gy", "gx"):
        n = lax.axis_size(axis)
        d = 1
        while d < n:
            y = lax.ppermute(x, axis, [(i, i ^ d) for i in range(n)])
            s, e = two_sum(x[:half], y[:half])
            x = jnp.concatenate([s, (x[half:] + y[half:]) + e])
            d *= 2
    return x


def params(limit=8):
    return pltpu.CompilerParams(vmem_limit_bytes=limit * 2**20)


def shape(*dims):
    return jax.ShapeDtypeStruct(dims, F32)


def body(rhs, stiffness, coupling, edges, flip, pinned):
    loads, _, height, width = rhs.shape
    ext = height + 24
    groups = loads // PER
    merged = (groups + 3) // 4
    main = rhs.reshape(loads * 3, height, width)
    raw = (stiffness, coupling, edges, flip, pinned)
    fields = loads * 3 + 18

    def end_block(x, at):
        block = x.shape[:-2] + (8, width)
        lead = (0,) * (x.ndim - 2)
        return pl.BlockSpec(block, lambda g: lead + (at, 0))

    low, high = pl.pallas_call(
        rows_kernel,
        grid=(1,),
        in_specs=[end_block(x, at) for at in (0, height // 8 - 1) for x in (main,) + raw],
        out_specs=[pl.BlockSpec((fields * HALO, width), lambda g: (0, 0))] * 2,
        out_shape=[shape(fields * HALO, width)] * 2,
        compiler_params=params(),
    )(main, *raw, main, *raw)
    up = moved(low, "gx", -1)
    down = moved(high, "gx", 1)

    count = merged + 2
    wide = 4 * 3 * PER

    def send_columns(kernel, in_specs, rows, scratch, *operands):
        part = pl.BlockSpec((1, 3, rows, width), lambda h: (h, 0, 0, 0))
        right, left = pl.pallas_call(
            kernel,
            grid=(count,),
            in_specs=in_specs,
            out_specs=[part] * 2,
            out_shape=[shape(count, 3, rows, width)] * 2,
            scratch_shapes=scratch,
            compiler_params=params(),
        )(*operands)
        return moved(right, "gy", 1), moved(left, "gy", -1)

    resident = pl.BlockSpec(memory_space=pltpu.VMEM)
    from_left, from_right = send_columns(
        functools.partial(columns_kernel, merged, height),
        [pl.BlockSpec((wide, height, width), lambda h: (jnp.minimum(h, merged - 1), 0, 0))] + [resident] * 5,
        height, [], main, *raw,
    )
    line = pl.BlockSpec((wide * HALO, width), lambda h: (jnp.minimum(h, merged - 1), 0))
    left_ends, right_ends = send_columns(
        functools.partial(ends_kernel, merged, loads * 3),
        [line] * 2 + [resident] * 2,
        16, [pltpu.VMEM((8, width), F32)], down, up, down, up,
    )
    cm, cs = pl.pallas_call(
        functools.partial(prepare_kernel, loads, merged),
        out_shape=[shape(NCOEF, ext, width), shape(NCOEF, ext, width)],
        scratch_shapes=[pltpu.VMEM((6, 3, ext, width), F32)] * 2 + [pltpu.VMEM((2, 3, ext, width), F32)],
        compiler_params=params(),
    )(*raw, up, down, from_left, from_right, left_ends, right_ends)

    own_tile = pl.BlockSpec((3 * PER, height, width), lambda g: (g, 0, 0))
    line = pl.BlockSpec((3 * PER * HALO, width), lambda g: (g, 0))
    quarter = pl.BlockSpec((1, 3, height, width), lambda g: (g // 4, 0, 0, 0))
    corner = pl.BlockSpec((1, 3, 16, width), lambda g: (g // 4, 0, 0, 0))
    part = pl.BlockSpec((16, 128), lambda g: (0, 0))
    tiles = pltpu.VMEM((loads * 3, ext, width), F32)
    strips = pltpu.VMEM((groups, 3, ext, width), F32)
    own_shape = shape(loads * 3, height, width)
    sums_shape = shape(16, 128)
    sums_buffer = pltpu.VMEM((7, 128, 128), F32)
    small = [pltpu.VMEM((PAIR, 3, ext, width), F32), pltpu.VMEM((3, ext, width), F32)]
    u0, u1, u2, u3, s0, s1, s2, s3, sums = pl.pallas_call(
        functools.partial(first_kernel, height),
        grid=(groups,),
        in_specs=[own_tile, line, line, quarter, quarter] + [corner] * 2 + [resident] * 2,
        out_specs=[resident] * 8 + [part],
        out_shape=[tiles] * 4 + [strips] * 4 + [sums_shape],
        scratch_shapes=small + [pltpu.VMEM((2, 3, ext, width), F32), sums_buffer],
        compiler_params=params(),
    )(main, up, down, from_left, from_right, left_ends, right_ends, cm, cs)
    totals = summed(sums)
    fixed = part
    kept = pl.BlockSpec((32, 128), lambda g: (0, 0))
    w0, w1, w2, w3, sums, keep = pl.pallas_call(
        functools.partial(second_kernel, height),
        grid=(groups,),
        in_specs=[fixed] + [resident] * 10,
        out_specs=[resident] * 4 + [part, kept],
        out_shape=[tiles] * 4 + [sums_shape, shape(32, 128)],
        scratch_shapes=small + [pltpu.VMEM((128, 128), F32)] * 2 + [pltpu.VMEM((3, ext, width), F32)] * 3
        + [sums_buffer],
        compiler_params=params(),
    )(totals, u0, u1, u2, u3, s0, s1, s2, s3, cm, cs)
    totals = summed(sums)
    x, r = pl.pallas_call(
        functools.partial(last_kernel, height),
        grid=(groups,),
        in_specs=[fixed, kept, own_tile] + [resident] * 7,
        out_specs=[own_tile] * 2,
        out_shape=[own_shape] * 2,
        scratch_shapes=[pltpu.VMEM((32, 128), F32), pltpu.VMEM((128, 128), F32), pltpu.VMEM((128, 128), F32)],
        compiler_params=params(),
    )(totals, keep, main, u0, u1, u2, w0, w1, w2, w3)
    return x.reshape(rhs.shape), r.reshape(rhs.shape)


def solution(mesh):
    placed = (
        P(None, None, "gx", "gy"),
        P(None, "gx", "gy"),
        P(None, "gx", "gy"),
        P(None, "gx", "gy"),
        P("gx", "gy"),
        P("gx", "gy"),
    )
    return jax.shard_map(
        body,
        mesh=mesh,
        in_specs=placed,
        out_specs=(P(None, None, "gx", "gy"), P(None, None, "gx", "gy")),
        check_vma=False,
    )
```

```python
import functools
import jax
import jax.numpy as jnp
from jax import lax
from jax.experimental import pallas as pl
from jax.experimental.pallas import tpu as pltpu
from jax.sharding import PartitionSpec as P

DAMP = 0.2
HALO = 6
TOP = 12
PITCH = 32
PER = 4
NCOEF = 20
PAIR = 2
F32 = jnp.float32


def two_sum(a, b):
    s = a + b
    t = s - a
    return s, (a - (s - t)) + (b - t)


def quick(a, b):
    s = a + b
    return s, b - (s - a)


def halves(a):
    t = 4097.0 * a
    high = t - (t - a)
    return high, a - high


def two_mul(a, b):
    p = a * b
    ah, al = halves(a)
    bh, bl = halves(b)
    return p, ((ah * bh - p) + ah * bl + al * bh) + al * bl


def dd_add(x, y):
    s, e = two_sum(x[0], y[0])
    return quick(s, e + (x[1] + y[1]))


def dd_neg(x):
    return -x[0], -x[1]


def dd_sub(x, y):
    return dd_add(x, dd_neg(y))


def dd_mul(x, y):
    p, e = two_mul(x[0], y[0])
    return quick(p, e + (x[0] * y[1] + x[1] * y[0]))


def dd_div(x, y):
    q = x[0] / y[0]
    p, e = two_mul(q, y[0])
    rest = ((x[0] - p) - e) + (x[1] - q * y[1])
    return quick(q, rest / y[0])


def lift(x):
    return x, jnp.zeros_like(x)


def dd_fma(x, a, y):
    return dd_sub(x, dd_mul(a, y))


def first_block(m):
    one = [dd_div(m[1], m[0])]
    a0 = one[0]
    s1 = {l: dd_fma(m[l + 1], a0, m[l]) for l in range(1, 5)}
    q1 = dd_div(s1[2], s1[1])
    a1 = dd_sub(q1, a0)
    b1 = dd_div(s1[1], m[0])
    s2 = {l: dd_fma(dd_fma(s1[l + 1], a1, s1[l]), b1, m[l]) for l in range(2, 4)}
    a2 = dd_sub(dd_div(s2[3], s2[2]), q1)
    b2 = dd_div(s2[2], s1[1])
    return (a0, a1, a2), (b1, b2), s2[2]


def second_block(nu, a, b, b3):
    a0, a1, a2 = a
    b1, b2 = b
    t2 = {1: nu[0]}
    t2[2] = dd_add(nu[1], dd_mul(a2, t2[1]))
    t12 = nu[0]
    t2[3] = dd_add(dd_add(nu[2], dd_mul(a2, t2[2])), dd_mul(b2, t12))
    t13 = dd_add(t2[2], dd_mul(a1, t12))
    t2[4] = dd_add(dd_add(nu[3], dd_mul(a2, t2[3])), dd_mul(b2, t13))
    a3 = dd_div(nu[1], nu[0])
    t4 = {j: dd_fma(dd_fma(nu[j + 1], a3, nu[j]), b3, t2[j]) for j in range(1, 5)}
    b4 = dd_div(t4[1], nu[0])
    q4 = dd_div(t4[2], t4[1])
    a4 = dd_sub(q4, a3)
    t5 = {j: dd_fma(dd_fma(t4[j + 1], a4, t4[j]), b4, nu[j]) for j in (2, 3)}
    b5 = dd_div(t5[2], t4[1])
    a5 = dd_sub(dd_div(t5[3], t5[2]), q4)
    return (a3, a4, a5), (b4, b5)


def steps_of(a, b, before):
    alphas, sigmas = [], []
    for ak, bk in zip(a, b):
        if before is None:
            alpha = 1.0 / (ak + DAMP)
            sigma = jnp.zeros_like(alpha)
        else:
            ratio = bk * before
            alpha = 1.0 / (ak + DAMP - ratio)
            sigma = alpha * ratio
        alphas.append(alpha)
        sigmas.append(sigma)
        before = alpha
    return alphas, sigmas


def early_residuals(alphas, sigmas):
    one = jnp.ones_like(alphas[0])
    zero = jnp.zeros_like(one)
    polys = [[one, zero, zero, zero]]
    pins = [one]
    for k in range(3):
        now = polys[-1]
        old = polys[-2] if k else [zero] * 4
        lead = 1.0 + sigmas[k] - DAMP * alphas[k]
        polys.append([
            lead * now[i] - (alphas[k] * now[i - 1] if i else zero) - sigmas[k] * old[i]
            for i in range(4)
        ])
        pins.append((1.0 + sigmas[k] - alphas[k]) * pins[-1] - (sigmas[k] * pins[-2] if k else zero))
    return polys, pins


PIN = 1.0 - DAMP


def with_pins(sums, weight):
    out = []
    factor = 1.0
    for k in range(6):
        out.append(dd_add(sums[k], dd_mul(weight, lift(jnp.full_like(weight[0], factor)))))
        factor *= PIN
    return out


def row(ref, i):
    return ref[i:i + 1, :]


def pair_sums(parts_ref):
    def step(d, total):
        high, low = total
        high, error = two_sum(high, parts_ref[d])
        return high, low + error
    zero = jnp.zeros(parts_ref.shape[1:], F32)
    high, low = lax.fori_loop(1, parts_ref.shape[0], step, (parts_ref[0], zero))
    return [quick(high[i:i + 1, :], low[i:i + 1, :]) for i in range(7)]


def middle_scalars(parts_ref, keep_ref):
    sums = pair_sums(parts_ref)
    m = with_pins(sums, sums[6])
    a, b, top = first_block(m)
    alphas, sigmas = steps_of([x[0] for x in a], [None] + [x[0] for x in b], None)
    polys, pins = early_residuals(alphas, sigmas)
    lead = alphas[0] * alphas[1] * alphas[2]
    values = list(polys[3]) + [pins[3], pins[2]]
    values += [x for pair in a + b for x in pair]
    values += [top[0], sums[6][0]] + alphas + sigmas + [lead]
    for i, value in enumerate(values):
        keep_ref[i:i + 1, :] = value


def last_scalars(keep_ref, parts_ref, out_ref):
    kept = [row(keep_ref, i) for i in range(25)]
    pins = [kept[5], kept[4]]
    a = [(kept[6 + 2 * i], kept[7 + 2 * i]) for i in range(3)]
    b = [(kept[12 + 2 * i], kept[13 + 2 * i]) for i in range(2)]
    top, weight = kept[16], kept[17]
    alphas, sigmas = kept[18:21], kept[21:24]
    lead = kept[24]
    nu = with_pins(pair_sums(parts_ref), lift(weight * kept[4] * kept[4]))
    b3 = dd_div(nu[0], dd_mul(lift(top), dd_mul(lift(lead), lift(lead))))
    a_late, b_late = second_block(nu, a, b, b3)
    more, more_sigmas = steps_of(
        [x[0] for x in a_late], [b3[0]] + [x[0] for x in b_late], alphas[2]
    )
    alphas = alphas + more
    sigmas = sigmas + more_sigmas
    one = jnp.ones_like(top)
    zero = jnp.zeros_like(top)

    def unit(i):
        return [one if j == i else zero for j in range(7)]

    def scale(f, v):
        return [f * x for x in v]

    def plus(*vs):
        total = list(vs[0])
        for v in vs[1:]:
            total = [p + q for p, q in zip(total, v)]
        return total

    residuals = [unit(0), unit(1), unit(2), unit(3)]

    def times_h(v):
        out = [zero] * 7
        for k in range(3):
            image = scale((1.0 + sigmas[k]) / alphas[k] - DAMP, unit(k))
            image[k + 1] = image[k + 1] - 1.0 / alphas[k]
            if k:
                image[k - 1] = image[k - 1] - sigmas[k] / alphas[k]
            out = plus(out, scale(v[k], image))
        for k in range(3, 6):
            out[k + 1] = out[k + 1] + v[k]
        return out

    for k in range(3, 6):
        now, old = residuals[k], residuals[k - 1]
        residuals.append(plus(
            scale(1.0 + sigmas[k] - DAMP * alphas[k], now),
            scale(-alphas[k], times_h(now)),
            scale(-sigmas[k], old),
        ))
        pins.append((1.0 + sigmas[k] - alphas[k]) * pins[-1] - sigmas[k] * pins[-2])
    answers = [[zero] * 7, scale(alphas[0], unit(0))]
    for k in range(1, 6):
        answers.append(plus(
            scale(1.0 + sigmas[k], answers[k]), scale(alphas[k], residuals[k]), scale(-sigmas[k], answers[k - 1])
        ))
    polys, early = early_residuals(alphas[:3], sigmas[:3])
    pins_all = early[:3] + pins[1:]
    pin_answers = [zero, alphas[0]]
    for k in range(1, 6):
        pin_answers.append(
            (1.0 + sigmas[k]) * pin_answers[k] + alphas[k] * pins_all[k] - sigmas[k] * pin_answers[k - 1]
        )
    rows = []
    for v, pin in ((answers[6], pin_answers[6]), (residuals[6], pins_all[6])):
        for i in range(3):
            rows.append(v[0] * polys[0][i] + v[1] * polys[1][i] + v[2] * polys[2][i])
        rows += v[3:] + [pin]
    for i, value in enumerate(rows):
        out_ref[i:i + 1, :] = value


def lanes(rows=8):
    return lax.broadcasted_iota(jnp.int32, (rows, 128), 1)


def field(refs, i, rows):
    stiffness, coupling, edges, flip, pinned = refs
    if i < 2:
        return stiffness[i, rows, :]
    if i < 4:
        return coupling[i - 2, rows, :]
    if i < 16:
        return edges[i - 4, rows, :]
    if i == 16:
        return flip[rows, :].astype(F32)
    return (1 - pinned[rows, :]).astype(F32)


def join_rows(dst, lead, own, up, down, height):
    ext = dst.shape[-2]
    dst[lead + (slice(0, 8),)] = jnp.zeros((8, 128), F32)
    dst[lead + (slice(ext - 8, ext),)] = jnp.zeros((8, 128), F32)
    dst[lead + (slice(TOP, TOP + height),)] = own
    dst[lead + (slice(TOP - HALO, TOP),)] = down
    dst[lead + (slice(TOP + height, TOP + height + HALO),)] = up


def own_columns(x, i, kept):
    lane = lanes() % PITCH
    here = lanes() // PITCH == i
    kept = jnp.where(here & (lane >= 6) & (lane < 12), pltpu.roll(x, PITCH * i + 6, 1), kept)
    return jnp.where(here & (lane >= 16) & (lane < 21), pltpu.roll(x, (PITCH * i + 16 - 123) % 128, 1), kept)


def other_columns(left, right, q, kept):
    lane = lanes() % PITCH
    kept = jnp.where(lane < HALO, pltpu.roll(left, (128 - 8 * q) % 128, 1), kept)
    return jnp.where(
        (lane >= 21) & (lane < 21 + HALO), pltpu.roll(right, (128 + 21 - 8 * q) % 128, 1), kept)


def join_sides(sides, column, lead, merged, corners, height):
    for n in range(2):
        join_rows(sides, (n, column), merged[n][lead + (slice(None),)], corners[n][lead + (slice(8, 8 + HALO),)],
                  corners[n][lead + (slice(0, HALO),)], height)


def prepare_kernel(loads, merged, stiffness, coupling, edges, flip, pinned, up_ref, down_ref, left_ref, right_ref, left_ends, right_ends,
                   main_out, strip_out, wide, strip, sides):
    refs = (stiffness, coupling, edges, flip, pinned)
    height = flip.shape[0]
    ext = wide.shape[2]
    for p in range(6):
        for c in range(3):
            k = 3 * (loads + p) + c
            join_rows(wide, (p, c), field(refs, 3 * p + c, slice(0, height)), up_ref[k * HALO:(k + 1) * HALO, :],
                      down_ref[k * HALO:(k + 1) * HALO, :], height)
            join_sides(sides, c, (merged + p // 4, c), (left_ref, right_ref), (left_ends, right_ends), height)
            for r in range(0, ext, 8):
                x = wide[p, c, r:r + 8, :]
                total = jnp.zeros((8, 128), F32)
                for i in range(PER):
                    total = own_columns(x, i, total)
                strip[p, c, r:r + 8, :] = other_columns(
                    sides[0, c, r:r + 8, :], sides[1, c, r:r + 8, :], p % 4, total)
    lane = lax.broadcasted_iota(jnp.int32, (ext, 128), 1)
    line = lax.broadcasted_iota(jnp.int32, (ext, 128), 0)
    near = None
    for which, (src, dst) in enumerate(((strip, strip_out), (wide, main_out))):
        def raw(i):
            return src[i // 3, i % 3]
        flipped = raw(16) > 0.5
        zero = jnp.zeros((ext, 128), F32)
        k1, k2 = raw(0), raw(1)
        root1, root2 = jnp.sqrt(raw(2)), jnp.sqrt(raw(3))
        other = jnp.where(flipped, zero, k2)
        left = pltpu.roll(other, 1, 1)
        if which == 1:
            left = jnp.where(lane == 0, near, left)
        else:
            near = pltpu.roll(other, 128 - (HALO - 1), 1)
        below = jnp.where(line == 0, zero, pltpu.roll(other, 1, 0))
        dst[0] = k1 + left
        dst[1] = jnp.where(flipped, k2, k1) + below
        dst[2] = jnp.where(flipped, k1 + k2, zero)
        for c in range(3):
            dst[3 + c] = root1 * raw(4 + c)
            dst[6 + c] = root1 * raw(7 + c)
            one = root2 * raw(10 + c)
            two = root2 * raw(13 + c)
            dst[9 + c] = jnp.where(flipped, zero, two)
            dst[12 + c] = jnp.where(flipped, two, one)
            dst[15 + c] = jnp.where(flipped, one, -(one + two))
        dst[18] = raw(16)
        dst[19] = raw(17)


def dot3(p, q):
    return p[0] * q[0] + p[1] * q[1] + p[2] * q[2]


def tile_step(tiles, coef, first, chunks):
    stop = first + 8 * chunks
    for r in list(range(first, stop, 8)) + [stop - 7]:
        for side, get, beside, _, _, _ in tiles:
            for c in range(3):
                side[c, r:r + 8, :] = beside(c, r, get(c, r))
    top = lax.broadcasted_iota(jnp.int32, (8, 128), 0) == 0
    before = [None] * len(tiles)
    for r in range(first, stop, 8):
        def co(i):
            return coef[i, r:r + 8, :]
        flipped = co(18) > 0.5
        g1 = [co(3 + c) for c in range(3)]
        g2 = [co(6 + c) for c in range(3)]
        hb = [co(9 + c) for c in range(3)]
        hc = [co(12 + c) for c in range(3)]
        hd = [co(15 + c) for c in range(3)]
        wv, wh, wd, free = co(0), co(1), co(2), co(19)
        forces = []
        for side, get, _, _, _, _ in tiles:
            base = [get(c, r) for c in range(3)]
            eb = [get(c, r + 1) - base[c] for c in range(3)]
            ec = [side[c, r:r + 8, :] - base[c] for c in range(3)]
            ed = [side[c, r + 1:r + 9, :] - base[c] for c in range(3)]
            ex = [jnp.where(flipped, ed[c], ec[c]) for c in range(3)]
            s1 = dot3(g1, eb) + dot3(g2, ex)
            s2 = dot3(hb, eb) + dot3(hc, ec) + dot3(hd, ed)
            zero = jnp.zeros_like(s1)
            s1c = jnp.where(flipped, zero, s1)
            s1d = jnp.where(flipped, s1, zero)
            forces.append([(
                wv * eb[c] + s1 * g1[c] + s2 * hb[c],
                wh * ec[c] + s1c * g2[c] + s2 * hc[c],
                wd * ed[c] + s1d * g2[c] + s2 * hd[c],
            ) for c in range(3)])
        for n, (_, _, _, spill, put, put_spill) in enumerate(tiles):
            rolled = []
            for c in range(3):
                fb, fc, fd = forces[n][c]
                down_b, down_d = pltpu.roll(fb, 1, 0), pltpu.roll(fd, 1, 0)
                rolled.append((down_b, down_d))
                if before[n] is not None:
                    down_b = jnp.where(top, before[n][c][0], down_b)
                    down_d = jnp.where(top, before[n][c][1], down_d)
                own = down_b - (fb + fc + fd)
                q = fc + down_d
                if put_spill is not None:
                    put_spill(c, r, q)
                put(c, r, free * (own + spill(c, r, q)))
            before[n] = rolled


def apply_groups(src_mains, src_strips, dst_mains, dst_strips, coef_main, coef_strip, scratch, first, chunks):
    side, strip_q = scratch
    lane = lanes()

    def strip_tile(n):
        def put(c, r, x):
            if dst_strips is not None:
                dst_strips[n][c, r:r + 8, :] = x

        def put_q(c, r, x):
            strip_q[n, c, r:r + 8, :] = x

        return (
            side.at[n],
            lambda c, r: src_strips[n][c, r:r + 8, :],
            lambda c, r, x: pltpu.roll(x, 127, 1),
            lambda c, r, x: pltpu.roll(x, 1, 1),
            put,
            put_q,
        )

    tile_step([strip_tile(n) for n in range(PAIR)], coef_strip, first, chunks)

    def tile(n, i, slot):
        base = 3 * i
        to_last = (127 - (PITCH * i + 21)) % 128
        to_first = (128 - (PITCH * i + HALO - 1)) % 128

        def get(c, r):
            return src_mains[n][base + c, r:r + 8, :]

        def beside(c, r, x):
            beyond = pltpu.roll(src_strips[n][c, r:r + 8, :], to_last, 1)
            return jnp.where(lane == 127, beyond, pltpu.roll(x, 127, 1))

        def spill(c, r, x):
            beyond = pltpu.roll(strip_q[n, c, r:r + 8, :], to_first, 1)
            return jnp.where(lane == 0, beyond, pltpu.roll(x, 1, 1))

        def put(c, r, x):
            dst_mains[n][base + c, r:r + 8, :] = x

        return side.at[slot], get, beside, spill, put, None

    for n in range(PAIR):
        for i in range(0, PER, PAIR):
            tile_step([tile(n, i + j, j) for j in range(PAIR)], coef_main, first, chunks)


def add_up(sums, totals_ref):
    totals_ref[...] = jnp.zeros(totals_ref.shape, F32)
    for k in range(7):
        totals_ref[k:k + 1, :] = jnp.sum(sums[k].T, axis=0, keepdims=True)


def fold(x):
    return jnp.sum(x, axis=0, keepdims=True)


def inner(p_ref, q_ref, i, p_at, q_at, height):
    total = None
    for c in range(3):
        for r in range(0, height, 8):
            t = p_ref[3 * i + c, p_at + r:p_at + r + 8, :] * q_ref[3 * i + c, q_at + r:q_at + r + 8, :]
            total = t if total is None else total + t
    return fold(total)


def mine(ref, groups):
    return [ref.at[pl.ds(g * 3 * PER, 3 * PER)] for g in groups]


def clear(scratch):
    for ref in scratch:
        ref[...] = jnp.zeros(ref.shape, F32)


def first_kernel(height, rhs_ref, up_ref, down_ref, left_ref, right_ref, left_ends, right_ends, cm, cs,
                 u0_all, u1_all, u2_all, u3_all, s0_all, s1_all, s2_all, s3_all, totals_out, side, strip_q, sides, sums):
    scratch = (side, strip_q)
    group = pl.program_id(0)
    ext = cm.shape[1]

    @pl.when(group == 0)
    def _():
        clear(scratch)
        clear((sums,))

    groups = [group * PAIR + n for n in range(PAIR)]
    chain = [mine(ref, groups) for ref in (u0_all, u1_all, u2_all, u3_all)]
    strips = [[ref.at[g] for g in groups] for ref in (s0_all, s1_all, s2_all, s3_all)]
    for n, g in enumerate(groups):
        u0, s0 = chain[0][n], strips[0][n]
        for c in range(3):
            join_sides(sides, c, (0, c), (left_ref, right_ref), (left_ends, right_ends), height)
            for i in range(PER):
                k = 3 * (n * PER + i) + c
                join_rows(u0, (3 * i + c,), rhs_ref[k, :, :], up_ref[k * HALO:(k + 1) * HALO, :],
                          down_ref[k * HALO:(k + 1) * HALO, :], height)
            for r in range(0, ext, 8):
                total = jnp.zeros((8, 128), F32)
                for i in range(PER):
                    x = u0[3 * i + c, r:r + 8, :] * cm[19, r:r + 8, :]
                    u0[3 * i + c, r:r + 8, :] = x
                    total = own_columns(x, i, total)
                total = other_columns(sides[0, c, r:r + 8, :], sides[1, c, r:r + 8, :], g % 4, total)
                s0[c, r:r + 8, :] = total * cs[19, r:r + 8, :]
    for j, (first, rows) in enumerate(((TOP - 6, height + 16), (TOP - 5, height + 16), (TOP - 4, height + 8))):
        apply_groups(chain[j], strips[j], chain[j + 1], strips[j + 1], cm, cs, scratch, first, rows // 8)
    for n, g in enumerate(groups):
        vectors = [v[n] for v in chain]
        for i in range(PER):
            rows = [inner(vectors[k // 2], vectors[(k + 1) // 2], i, TOP, TOP, height) for k in range(6)]
            total = None
            for c in range(3):
                for r in range(0, height, 8):
                    t = rhs_ref[3 * (n * PER + i) + c, r:r + 8, :] - vectors[0][3 * i + c, TOP + r:TOP + r + 8, :]
                    t = t * t
                    total = t if total is None else total + t
            rows.append(fold(total))
            for k in range(7):
                sums[k, pl.ds(g * PER + i, 1), :] = rows[k]

    @pl.when(group == pl.num_programs(0) - 1)
    def _():
        add_up(sums, totals_out)


def spread(table, load, i):
    return jnp.broadcast_to(table[pl.ds(load, 1), i:i + 1], (8, 128))


def transposed(keep, square, table):
    square[...] = jnp.zeros((128, 128), F32)
    square[0:32, :] = keep[...]
    table[...] = square[...].T


def second_kernel(height, totals_ref, u0_all, u1_all, u2_all, u3_all, s0_all, s1_all, s2_all, s3_all, cm, cs,
                  w0_all, w1_all, w2_all, w3_all, totals_out, keep_ref, side, strip_q, square, table, t0, t1, t2, sums):
    scratch = (side, strip_q)
    group = pl.program_id(0)

    @pl.when(group == 0)
    def _():
        clear(scratch)
        clear((sums,))
        keep_ref[...] = jnp.zeros(keep_ref.shape, F32)
        middle_scalars(totals_ref, keep_ref)
        transposed(keep_ref, square, table)

    groups = [group * PAIR + n for n in range(PAIR)]
    early = [mine(ref, groups) for ref in (u0_all, u1_all, u2_all, u3_all)]
    chain = [mine(ref, groups) for ref in (w0_all, w1_all, w2_all, w3_all)]
    strips = [[ref.at[g] for g in groups] for ref in (s0_all, s1_all, s2_all, s3_all)]
    chunks = (height + 8) // 8
    window = range(TOP - 4, TOP - 4 + 8 * chunks, 8)
    segment = lanes() // PITCH
    for n, g in enumerate(groups):
        weights = [[spread(table, g * PER + i, j) for j in range(4)] for i in range(PER)]
        for i in range(PER):
            for c in range(3):
                for r in window:
                    x = weights[i][0] * early[0][n][3 * i + c, r:r + 8, :]
                    for j in range(1, 4):
                        x = x + weights[i][j] * early[j][n][3 * i + c, r:r + 8, :]
                    chain[0][n][3 * i + c, r:r + 8, :] = x
        mixed = []
        for j in range(4):
            m = weights[0][j]
            for i in range(1, PER):
                m = jnp.where(segment == i, weights[i][j], m)
            mixed.append(m)
        for c in range(3):
            for r in window:
                x = mixed[0] * strips[0][n][c, r:r + 8, :]
                for j in range(1, 4):
                    x = x + mixed[j] * strips[j][n][c, r:r + 8, :]
                t0[n, c, r:r + 8, :] = x
    late = [[t.at[n] for n in range(PAIR)] for t in (t0, t1, t2)] + [None]
    for j in range(3):
        apply_groups(chain[j], late[j], chain[j + 1], late[j + 1], cm, cs, scratch, TOP - 4, chunks)
    for n, g in enumerate(groups):
        vectors = [v[n] for v in chain]
        for i in range(PER):
            for k in range(6):
                sums[k, pl.ds(g * PER + i, 1), :] = inner(
                    vectors[k // 2], vectors[(k + 1) // 2], i, TOP, TOP, height)

    @pl.when(group == pl.num_programs(0) - 1)
    def _():
        add_up(sums, totals_out)


def last_kernel(height, totals_ref, keep_ref, rhs_ref, u0_all, u1_all, u2_all, w0_all, w1_all, w2_all, w3_all,
                x_ref, r_ref, rows, square, table):
    group = pl.program_id(0)

    @pl.when(group == 0)
    def _():
        rows[...] = jnp.zeros(rows.shape, F32)
        last_scalars(keep_ref, totals_ref, rows)
        transposed(rows, square, table)

    mine = pl.ds(group * 3 * PER, 3 * PER)
    basis = [ref.at[mine] for ref in (u0_all, u1_all, u2_all, w0_all, w1_all, w2_all, w3_all)]
    for i in range(PER):
        f = [spread(table, group * PER + i, j) for j in range(16)]
        for c in range(3):
            k = 3 * i + c
            for r in range(0, height, 8):
                vectors = [ref[k, TOP + r:TOP + r + 8, :] for ref in basis]
                vectors.append(rhs_ref[k, r:r + 8, :] - vectors[0])
                for out, at in ((x_ref, 0), (r_ref, 8)):
                    total = f[at] * vectors[0]
                    for j in range(1, 8):
                        total = total + f[at + j] * vectors[j]
                    out[k, r:r + 8, :] = total


def rows_kernel(*refs):
    low_refs, high_refs, outs = refs[:6], refs[6:12], refs[12:]
    loads = low_refs[0].shape[0]
    for j in range(loads + 18):
        to = slice(j * HALO, (j + 1) * HALO)
        for source, rows, out in ((low_refs, slice(0, HALO), outs[0]), (high_refs, slice(8 - HALO, 8), outs[1])):
            if j < loads:
                out[to, :] = source[0][j, rows, :]
            else:
                out[to, :] = field(source[1:], j - loads, rows)


def cut(get, rows, quarters, right_ref, left_ref):
    lane = lanes() % PITCH
    segment = lanes() // PITCH
    for c in range(3):
        for r in rows:
            right = jnp.zeros((8, 128), F32)
            left = right
            for q in range(quarters):
                for i in range(PER):
                    spot = (segment == i) & (lane >= 8 * q) & (lane < 8 * q + HALO)
                    x = get(q, i, c, r)
                    right = jnp.where(spot, pltpu.roll(x, (PITCH * i + 8 * q + HALO) % 128, 1), right)
                    left = jnp.where(spot, pltpu.roll(x, (PITCH * i + 8 * q) % 128, 1), left)
            right_ref[0, c, r:r + 8, :] = right
            left_ref[0, c, r:r + 8, :] = left


def each_group(merged, load_rows, raw_rows, rows, outs):
    group = pl.program_id(0)

    @pl.when(group < merged)
    def _():
        cut(lambda q, i, c, r: load_rows(3 * (PER * q + i) + c, r), rows, 4, *outs)

    for p in (0, 4):
        @pl.when(group == merged + p // 4)
        def _():
            cut(lambda q, i, c, r: raw_rows(3 * (p + q) + c, r), rows, min(4, 6 - p), *outs)


def columns_kernel(merged, height, data_ref, *refs):
    each_group(
        merged, lambda k, r: data_ref[k, r:r + 8, :], lambda k, r: field(refs[:5], k, slice(r, r + 8)),
        range(0, height, 8), refs[5:],
    )


def ends_kernel(merged, fields, down_ref, up_ref, all_down, all_up, right_ref, left_ref, one):
    one[...] = jnp.zeros(one.shape, F32)

    def load_rows(k, r):
        one[0:HALO, :] = (down_ref, up_ref)[r // 8][k * HALO:(k + 1) * HALO, :]
        return one[...]

    def raw_rows(k, r):
        k = k + fields
        one[0:HALO, :] = (all_down, all_up)[r // 8][k * HALO:(k + 1) * HALO, :]
        return one[...]

    each_group(merged, load_rows, raw_rows, (0, 8), (right_ref, left_ref))


def moved(block, axis, distance):
    n = lax.axis_size(axis)
    return lax.ppermute(block, axis, [(i, i + distance) for i in range(n) if 0 <= i + distance < n])


def gathered(x):
    n = lax.axis_size("gx") * lax.axis_size("gy")
    return lax.all_to_all(jnp.broadcast_to(x[None], (n,) + x.shape), ("gx", "gy"), 0, 0, tiled=True)


def params(limit=8):
    return pltpu.CompilerParams(vmem_limit_bytes=limit * 2**20)


def shape(*dims):
    return jax.ShapeDtypeStruct(dims, F32)


def body(rhs, stiffness, coupling, edges, flip, pinned):
    loads, _, height, width = rhs.shape
    ext = height + 24
    groups = loads // PER
    merged = (groups + 3) // 4
    main = rhs.reshape(loads * 3, height, width)
    raw = (stiffness, coupling, edges, flip, pinned)
    fields = loads * 3 + 18

    def end_block(x, at):
        block = x.shape[:-2] + (8, width)
        lead = (0,) * (x.ndim - 2)
        return pl.BlockSpec(block, lambda g: lead + (at, 0))

    low, high = pl.pallas_call(
        rows_kernel,
        grid=(1,),
        in_specs=[end_block(x, at) for at in (0, height // 8 - 1) for x in (main,) + raw],
        out_specs=[pl.BlockSpec((fields * HALO, width), lambda g: (0, 0))] * 2,
        out_shape=[shape(fields * HALO, width)] * 2,
        compiler_params=params(60),
    )(main, *raw, main, *raw)
    up = moved(low, "gx", -1)
    down = moved(high, "gx", 1)

    count = merged + 2
    wide = 4 * 3 * PER

    def send_columns(kernel, in_specs, rows, scratch, *operands):
        part = pl.BlockSpec((1, 3, rows, width), lambda h: (h, 0, 0, 0))
        right, left = pl.pallas_call(
            kernel,
            grid=(count,),
            in_specs=in_specs,
            out_specs=[part] * 2,
            out_shape=[shape(count, 3, rows, width)] * 2,
            scratch_shapes=scratch,
            compiler_params=params(),
        )(*operands)
        return moved(right, "gy", 1), moved(left, "gy", -1)

    resident = pl.BlockSpec(memory_space=pltpu.VMEM)
    from_left, from_right = send_columns(
        functools.partial(columns_kernel, merged, height),
        [pl.BlockSpec((wide, height, width), lambda h: (jnp.minimum(h, merged - 1), 0, 0))] + [resident] * 5,
        height, [], main, *raw,
    )
    line = pl.BlockSpec((wide * HALO, width), lambda h: (jnp.minimum(h, merged - 1), 0))
    left_ends, right_ends = send_columns(
        functools.partial(ends_kernel, merged, loads * 3),
        [line] * 2 + [resident] * 2,
        16, [pltpu.VMEM((8, width), F32)], down, up, down, up,
    )
    cm, cs = pl.pallas_call(
        functools.partial(prepare_kernel, loads, merged),
        out_shape=[shape(NCOEF, ext, width), shape(NCOEF, ext, width)],
        scratch_shapes=[pltpu.VMEM((6, 3, ext, width), F32)] * 2 + [pltpu.VMEM((2, 3, ext, width), F32)],
        compiler_params=params(),
    )(*raw, up, down, from_left, from_right, left_ends, right_ends)

    own_tile = pl.BlockSpec((3 * PER, height, width), lambda g: (g, 0, 0))
    own_tiles = pl.BlockSpec((3 * PER * PAIR, height, width), lambda g: (g, 0, 0))
    line = pl.BlockSpec((3 * PER * PAIR * HALO, width), lambda g: (g, 0))
    quarter = pl.BlockSpec((1, 3, height, width), lambda g: (PAIR * g // 4, 0, 0, 0))
    corner = pl.BlockSpec((1, 3, 16, width), lambda g: (PAIR * g // 4, 0, 0, 0))
    part = pl.BlockSpec((8, 128), lambda g: (0, 0))
    tiles = pltpu.VMEM((loads * 3, ext, width), F32)
    strips = pltpu.VMEM((groups, 3, ext, width), F32)
    own_shape = shape(loads * 3, height, width)
    sums_shape = shape(8, 128)
    sums_buffer = pltpu.VMEM((7, 128, 128), F32)
    small = [pltpu.VMEM((PAIR, 3, ext, width), F32)] * 2
    u0, u1, u2, u3, s0, s1, s2, s3, sums = pl.pallas_call(
        functools.partial(first_kernel, height),
        grid=(groups // PAIR,),
        in_specs=[own_tiles, line, line, quarter, quarter] + [corner] * 2 + [resident] * 2,
        out_specs=[resident] * 8 + [part],
        out_shape=[tiles] * 4 + [strips] * 4 + [sums_shape],
        scratch_shapes=small + [pltpu.VMEM((2, 3, ext, width), F32), sums_buffer],
        compiler_params=params(),
    )(main, up, down, from_left, from_right, left_ends, right_ends, cm, cs)
    totals = gathered(sums)
    fixed = resident
    kept = pl.BlockSpec((32, 128), lambda g: (0, 0))
    w0, w1, w2, w3, sums, keep = pl.pallas_call(
        functools.partial(second_kernel, height),
        grid=(groups // PAIR,),
        in_specs=[fixed] + [resident] * 10,
        out_specs=[resident] * 4 + [part, kept],
        out_shape=[tiles] * 4 + [sums_shape, shape(32, 128)],
        scratch_shapes=small + [pltpu.VMEM((128, 128), F32)] * 2 + [pltpu.VMEM((PAIR, 3, ext, width), F32)] * 3
        + [sums_buffer],
        compiler_params=params(),
    )(totals, u0, u1, u2, u3, s0, s1, s2, s3, cm, cs)
    totals = gathered(sums)
    x, r = pl.pallas_call(
        functools.partial(last_kernel, height),
        grid=(groups,),
        in_specs=[fixed, kept, own_tile] + [resident] * 7,
        out_specs=[own_tile] * 2,
        out_shape=[own_shape] * 2,
        scratch_shapes=[pltpu.VMEM((32, 128), F32), pltpu.VMEM((128, 128), F32), pltpu.VMEM((128, 128), F32)],
        compiler_params=params(),
    )(totals, keep, main, u0, u1, u2, w0, w1, w2, w3)
    return x.reshape(rhs.shape), r.reshape(rhs.shape)


def solution(mesh):
    placed = (
        P(None, None, "gx", "gy"),
        P(None, "gx", "gy"),
        P(None, "gx", "gy"),
        P(None, "gx", "gy"),
        P("gx", "gy"),
        P("gx", "gy"),
    )
    return jax.shard_map(
        body,
        mesh=mesh,
        in_specs=placed,
        out_specs=(P(None, None, "gx", "gy"), P(None, None, "gx", "gy")),
        check_vma=False,
    )
```

```python
import functools
import jax
import jax.numpy as jnp
from jax import lax
from jax.experimental import pallas as pl
from jax.experimental.pallas import tpu as pltpu
from jax.sharding import PartitionSpec as P

DAMP = 0.2
HALO = 6
TOP = 12
PITCH = 32
PER = 4
NCOEF = 20
PAIR = 2
F32 = jnp.float32


def two_sum(a, b):
    s = a + b
    t = s - a
    return s, (a - (s - t)) + (b - t)


def quick(a, b):
    s = a + b
    return s, b - (s - a)


def halves(a):
    t = 4097.0 * a
    high = t - (t - a)
    return high, a - high


def two_mul(a, b):
    p = a * b
    ah, al = halves(a)
    bh, bl = halves(b)
    return p, ((ah * bh - p) + ah * bl + al * bh) + al * bl


def dd_add(x, y):
    s, e = two_sum(x[0], y[0])
    return quick(s, e + (x[1] + y[1]))


def dd_neg(x):
    return -x[0], -x[1]


def dd_sub(x, y):
    return dd_add(x, dd_neg(y))


def dd_mul(x, y):
    p, e = two_mul(x[0], y[0])
    return quick(p, e + (x[0] * y[1] + x[1] * y[0]))


def dd_div(x, y):
    q = x[0] / y[0]
    p, e = two_mul(q, y[0])
    rest = ((x[0] - p) - e) + (x[1] - q * y[1])
    return quick(q, rest / y[0])


def lift(x):
    return x, jnp.zeros_like(x)


def dd_fma(x, a, y):
    return dd_sub(x, dd_mul(a, y))


def first_block(m):
    one = [dd_div(m[1], m[0])]
    a0 = one[0]
    s1 = {l: dd_fma(m[l + 1], a0, m[l]) for l in range(1, 5)}
    q1 = dd_div(s1[2], s1[1])
    a1 = dd_sub(q1, a0)
    b1 = dd_div(s1[1], m[0])
    s2 = {l: dd_fma(dd_fma(s1[l + 1], a1, s1[l]), b1, m[l]) for l in range(2, 4)}
    a2 = dd_sub(dd_div(s2[3], s2[2]), q1)
    b2 = dd_div(s2[2], s1[1])
    return (a0, a1, a2), (b1, b2), s2[2]


def second_block(nu, a, b, b3):
    a0, a1, a2 = a
    b1, b2 = b
    t2 = {1: nu[0]}
    t2[2] = dd_add(nu[1], dd_mul(a2, t2[1]))
    t12 = nu[0]
    t2[3] = dd_add(dd_add(nu[2], dd_mul(a2, t2[2])), dd_mul(b2, t12))
    t13 = dd_add(t2[2], dd_mul(a1, t12))
    t2[4] = dd_add(dd_add(nu[3], dd_mul(a2, t2[3])), dd_mul(b2, t13))
    a3 = dd_div(nu[1], nu[0])
    t4 = {j: dd_fma(dd_fma(nu[j + 1], a3, nu[j]), b3, t2[j]) for j in range(1, 5)}
    b4 = dd_div(t4[1], nu[0])
    q4 = dd_div(t4[2], t4[1])
    a4 = dd_sub(q4, a3)
    t5 = {j: dd_fma(dd_fma(t4[j + 1], a4, t4[j]), b4, nu[j]) for j in (2, 3)}
    b5 = dd_div(t5[2], t4[1])
    a5 = dd_sub(dd_div(t5[3], t5[2]), q4)
    return (a3, a4, a5), (b4, b5)


def steps_of(a, b, before):
    alphas, sigmas = [], []
    for ak, bk in zip(a, b):
        if before is None:
            alpha = 1.0 / (ak + DAMP)
            sigma = jnp.zeros_like(alpha)
        else:
            ratio = bk * before
            alpha = 1.0 / (ak + DAMP - ratio)
            sigma = alpha * ratio
        alphas.append(alpha)
        sigmas.append(sigma)
        before = alpha
    return alphas, sigmas


def early_residuals(alphas, sigmas):
    one = jnp.ones_like(alphas[0])
    zero = jnp.zeros_like(one)
    polys = [[one, zero, zero, zero]]
    pins = [one]
    for k in range(3):
        now = polys[-1]
        old = polys[-2] if k else [zero] * 4
        lead = 1.0 + sigmas[k] - DAMP * alphas[k]
        polys.append([
            lead * now[i] - (alphas[k] * now[i - 1] if i else zero) - sigmas[k] * old[i]
            for i in range(4)
        ])
        pins.append((1.0 + sigmas[k] - alphas[k]) * pins[-1] - (sigmas[k] * pins[-2] if k else zero))
    return polys, pins


PIN = 1.0 - DAMP


def with_pins(sums, weight):
    out = []
    factor = 1.0
    for k in range(6):
        out.append(dd_add(sums[k], dd_mul(weight, lift(jnp.full_like(weight[0], factor)))))
        factor *= PIN
    return out


def row(ref, i):
    return ref[i:i + 1, :]


def pair_sums(parts_ref):
    def step(d, total):
        high, low = total
        high, error = two_sum(high, parts_ref[d])
        return high, low + error
    zero = jnp.zeros(parts_ref.shape[1:], F32)
    high, low = lax.fori_loop(1, parts_ref.shape[0], step, (parts_ref[0], zero))
    return [quick(high[i:i + 1, :], low[i:i + 1, :]) for i in range(7)]


def middle_scalars(parts_ref, keep_ref):
    sums = pair_sums(parts_ref)
    m = with_pins(sums, sums[6])
    a, b, top = first_block(m)
    alphas, sigmas = steps_of([x[0] for x in a], [None] + [x[0] for x in b], None)
    polys, pins = early_residuals(alphas, sigmas)
    lead = alphas[0] * alphas[1] * alphas[2]
    values = list(polys[3]) + [pins[3], pins[2]]
    values += [x for pair in a + b for x in pair]
    values += [top[0], sums[6][0]] + alphas + sigmas + [lead]
    for i, value in enumerate(values):
        keep_ref[i:i + 1, :] = value


def last_scalars(keep_ref, parts_ref, out_ref):
    kept = [row(keep_ref, i) for i in range(25)]
    pins = [kept[5], kept[4]]
    a = [(kept[6 + 2 * i], kept[7 + 2 * i]) for i in range(3)]
    b = [(kept[12 + 2 * i], kept[13 + 2 * i]) for i in range(2)]
    top, weight = kept[16], kept[17]
    alphas, sigmas = kept[18:21], kept[21:24]
    lead = kept[24]
    nu = with_pins(pair_sums(parts_ref), lift(weight * kept[4] * kept[4]))
    b3 = dd_div(nu[0], dd_mul(lift(top), dd_mul(lift(lead), lift(lead))))
    a_late, b_late = second_block(nu, a, b, b3)
    more, more_sigmas = steps_of(
        [x[0] for x in a_late], [b3[0]] + [x[0] for x in b_late], alphas[2]
    )
    alphas = alphas + more
    sigmas = sigmas + more_sigmas
    one = jnp.ones_like(top)
    zero = jnp.zeros_like(top)

    def unit(i):
        return [one if j == i else zero for j in range(7)]

    def scale(f, v):
        return [f * x for x in v]

    def plus(*vs):
        total = list(vs[0])
        for v in vs[1:]:
            total = [p + q for p, q in zip(total, v)]
        return total

    residuals = [unit(0), unit(1), unit(2), unit(3)]

    def times_h(v):
        out = [zero] * 7
        for k in range(3):
            image = scale((1.0 + sigmas[k]) / alphas[k] - DAMP, unit(k))
            image[k + 1] = image[k + 1] - 1.0 / alphas[k]
            if k:
                image[k - 1] = image[k - 1] - sigmas[k] / alphas[k]
            out = plus(out, scale(v[k], image))
        for k in range(3, 6):
            out[k + 1] = out[k + 1] + v[k]
        return out

    for k in range(3, 6):
        now, old = residuals[k], residuals[k - 1]
        residuals.append(plus(
            scale(1.0 + sigmas[k] - DAMP * alphas[k], now),
            scale(-alphas[k], times_h(now)),
            scale(-sigmas[k], old),
        ))
        pins.append((1.0 + sigmas[k] - alphas[k]) * pins[-1] - sigmas[k] * pins[-2])
    answers = [[zero] * 7, scale(alphas[0], unit(0))]
    for k in range(1, 6):
        answers.append(plus(
            scale(1.0 + sigmas[k], answers[k]), scale(alphas[k], residuals[k]), scale(-sigmas[k], answers[k - 1])
        ))
    polys, early = early_residuals(alphas[:3], sigmas[:3])
    pins_all = early[:3] + pins[1:]
    pin_answers = [zero, alphas[0]]
    for k in range(1, 6):
        pin_answers.append(
            (1.0 + sigmas[k]) * pin_answers[k] + alphas[k] * pins_all[k] - sigmas[k] * pin_answers[k - 1]
        )
    rows = []
    for v, pin in ((answers[6], pin_answers[6]), (residuals[6], pins_all[6])):
        for i in range(3):
            rows.append(v[0] * polys[0][i] + v[1] * polys[1][i] + v[2] * polys[2][i])
        rows += v[3:] + [pin]
    for i, value in enumerate(rows):
        out_ref[i:i + 1, :] = value


def lanes(rows=8):
    return lax.broadcasted_iota(jnp.int32, (rows, 128), 1)


def field(refs, i, rows):
    stiffness, coupling, edges, flip, pinned = refs
    if i < 2:
        return stiffness[i, rows, :]
    if i < 4:
        return coupling[i - 2, rows, :]
    if i < 16:
        return edges[i - 4, rows, :]
    if i == 16:
        return flip[rows, :].astype(F32)
    return (1 - pinned[rows, :]).astype(F32)


def join_rows(dst, lead, own, up, down, height):
    ext = dst.shape[-2]
    dst[lead + (slice(0, 8),)] = jnp.zeros((8, 128), F32)
    dst[lead + (slice(ext - 8, ext),)] = jnp.zeros((8, 128), F32)
    dst[lead + (slice(TOP, TOP + height),)] = own
    dst[lead + (slice(TOP - HALO, TOP),)] = down
    dst[lead + (slice(TOP + height, TOP + height + HALO),)] = up


def own_columns(x, i, kept):
    lane = lanes() % PITCH
    here = lanes() // PITCH == i
    kept = jnp.where(here & (lane >= 6) & (lane < 12), pltpu.roll(x, PITCH * i + 6, 1), kept)
    return jnp.where(here & (lane >= 16) & (lane < 21), pltpu.roll(x, (PITCH * i + 16 - 123) % 128, 1), kept)


def other_columns(left, right, q, kept):
    lane = lanes() % PITCH
    kept = jnp.where(lane < HALO, pltpu.roll(left, (128 - 8 * q) % 128, 1), kept)
    return jnp.where(
        (lane >= 21) & (lane < 21 + HALO), pltpu.roll(right, (128 + 21 - 8 * q) % 128, 1), kept)


def join_sides(sides, column, lead, merged, corners, height):
    for n in range(2):
        join_rows(sides, (n, column), merged[n][lead + (slice(None),)], corners[n][lead + (slice(8, 8 + HALO),)],
                  corners[n][lead + (slice(0, HALO),)], height)


def prepare_kernel(loads, merged, stiffness, coupling, edges, flip, pinned, up_ref, down_ref, left_ref, right_ref, left_ends, right_ends,
                   main_out, strip_out, wide, strip, sides):
    refs = (stiffness, coupling, edges, flip, pinned)
    height = flip.shape[0]
    ext = wide.shape[2]
    for p in range(6):
        for c in range(3):
            k = 3 * (loads + p) + c
            join_rows(wide, (p, c), field(refs, 3 * p + c, slice(0, height)), up_ref[k * HALO:(k + 1) * HALO, :],
                      down_ref[k * HALO:(k + 1) * HALO, :], height)
            join_sides(sides, c, (merged + p // 4, c), (left_ref, right_ref), (left_ends, right_ends), height)
            for r in range(0, ext, 8):
                x = wide[p, c, r:r + 8, :]
                total = jnp.zeros((8, 128), F32)
                for i in range(PER):
                    total = own_columns(x, i, total)
                strip[p, c, r:r + 8, :] = other_columns(
                    sides[0, c, r:r + 8, :], sides[1, c, r:r + 8, :], p % 4, total)
    lane = lax.broadcasted_iota(jnp.int32, (ext, 128), 1)
    line = lax.broadcasted_iota(jnp.int32, (ext, 128), 0)
    near = None
    for which, (src, dst) in enumerate(((strip, strip_out), (wide, main_out))):
        def raw(i):
            return src[i // 3, i % 3]
        flipped = raw(16) > 0.5
        zero = jnp.zeros((ext, 128), F32)
        k1, k2 = raw(0), raw(1)
        root1, root2 = jnp.sqrt(raw(2)), jnp.sqrt(raw(3))
        other = jnp.where(flipped, zero, k2)
        left = pltpu.roll(other, 1, 1)
        if which == 1:
            left = jnp.where(lane == 0, near, left)
        else:
            near = pltpu.roll(other, 128 - (HALO - 1), 1)
        below = jnp.where(line == 0, zero, pltpu.roll(other, 1, 0))
        dst[0] = k1 + left
        dst[1] = jnp.where(flipped, k2, k1) + below
        dst[2] = jnp.where(flipped, k1 + k2, zero)
        for c in range(3):
            dst[3 + c] = root1 * raw(4 + c)
            dst[6 + c] = root1 * raw(7 + c)
            one = root2 * raw(10 + c)
            two = root2 * raw(13 + c)
            dst[9 + c] = jnp.where(flipped, zero, two)
            dst[12 + c] = jnp.where(flipped, two, one)
            dst[15 + c] = jnp.where(flipped, one, -(one + two))
        dst[18] = raw(16)
        dst[19] = raw(17)


def dot3(p, q):
    return p[0] * q[0] + p[1] * q[1] + p[2] * q[2]


def tile_step(tiles, coef, first, chunks):
    stop = first + 8 * chunks
    for r in list(range(first, stop, 8)) + [stop - 7]:
        for side, get, beside, _, _, _ in tiles:
            for c in range(3):
                side[c, r:r + 8, :] = beside(c, r, get(c, r))
    top = lax.broadcasted_iota(jnp.int32, (8, 128), 0) == 0
    before = [None] * len(tiles)
    for r in range(first, stop, 8):
        def co(i):
            return coef[i, r:r + 8, :]
        flipped = co(18) > 0.5
        g1 = [co(3 + c) for c in range(3)]
        g2 = [co(6 + c) for c in range(3)]
        hb = [co(9 + c) for c in range(3)]
        hc = [co(12 + c) for c in range(3)]
        hd = [co(15 + c) for c in range(3)]
        wv, wh, wd, free = co(0), co(1), co(2), co(19)
        forces = []
        for side, get, _, _, _, _ in tiles:
            base = [get(c, r) for c in range(3)]
            eb = [get(c, r + 1) - base[c] for c in range(3)]
            ec = [side[c, r:r + 8, :] - base[c] for c in range(3)]
            ed = [side[c, r + 1:r + 9, :] - base[c] for c in range(3)]
            ex = [jnp.where(flipped, ed[c], ec[c]) for c in range(3)]
            s1 = dot3(g1, eb) + dot3(g2, ex)
            s2 = dot3(hb, eb) + dot3(hc, ec) + dot3(hd, ed)
            zero = jnp.zeros_like(s1)
            s1c = jnp.where(flipped, zero, s1)
            s1d = jnp.where(flipped, s1, zero)
            forces.append([(
                wv * eb[c] + s1 * g1[c] + s2 * hb[c],
                wh * ec[c] + s1c * g2[c] + s2 * hc[c],
                wd * ed[c] + s1d * g2[c] + s2 * hd[c],
            ) for c in range(3)])
        for n, (_, _, _, spill, put, put_spill) in enumerate(tiles):
            rolled = []
            for c in range(3):
                fb, fc, fd = forces[n][c]
                down_b, down_d = pltpu.roll(fb, 1, 0), pltpu.roll(fd, 1, 0)
                rolled.append((down_b, down_d))
                if before[n] is not None:
                    down_b = jnp.where(top, before[n][c][0], down_b)
                    down_d = jnp.where(top, before[n][c][1], down_d)
                own = down_b - (fb + fc + fd)
                q = fc + down_d
                if put_spill is not None:
                    put_spill(c, r, q)
                put(c, r, free * (own + spill(c, r, q)))
            before[n] = rolled


def apply_groups(src_mains, src_strips, dst_mains, dst_strips, coef_main, coef_strip, scratch, first, chunks):
    side, strip_q = scratch
    lane = lanes()

    def strip_tile(n):
        def put(c, r, x):
            if dst_strips is not None:
                dst_strips[n][c, r:r + 8, :] = x

        def put_q(c, r, x):
            strip_q[n, c, r:r + 8, :] = x

        return (
            side.at[n],
            lambda c, r: src_strips[n][c, r:r + 8, :],
            lambda c, r, x: pltpu.roll(x, 127, 1),
            lambda c, r, x: pltpu.roll(x, 1, 1),
            put,
            put_q,
        )

    tile_step([strip_tile(n) for n in range(PAIR)], coef_strip, first, chunks)

    def tile(n, i, slot):
        base = 3 * i
        to_last = (127 - (PITCH * i + 21)) % 128
        to_first = (128 - (PITCH * i + HALO - 1)) % 128

        def get(c, r):
            return src_mains[n][base + c, r:r + 8, :]

        def beside(c, r, x):
            beyond = pltpu.roll(src_strips[n][c, r:r + 8, :], to_last, 1)
            return jnp.where(lane == 127, beyond, pltpu.roll(x, 127, 1))

        def spill(c, r, x):
            beyond = pltpu.roll(strip_q[n, c, r:r + 8, :], to_first, 1)
            return jnp.where(lane == 0, beyond, pltpu.roll(x, 1, 1))

        def put(c, r, x):
            dst_mains[n][base + c, r:r + 8, :] = x

        return side.at[slot], get, beside, spill, put, None

    for n in range(PAIR):
        for i in range(0, PER, PAIR):
            tile_step([tile(n, i + j, j) for j in range(PAIR)], coef_main, first, chunks)


def add_up(sums, totals_ref):
    totals_ref[...] = jnp.zeros(totals_ref.shape, F32)
    for k in range(7):
        totals_ref[k:k + 1, :] = jnp.sum(sums[k].T, axis=0, keepdims=True)


def fold(x):
    return jnp.sum(x, axis=0, keepdims=True)


def inner(p_ref, q_ref, i, p_at, q_at, height):
    total = None
    for c in range(3):
        for r in range(0, height, 8):
            t = p_ref[3 * i + c, p_at + r:p_at + r + 8, :] * q_ref[3 * i + c, q_at + r:q_at + r + 8, :]
            total = t if total is None else total + t
    return fold(total)


def mine(ref, groups):
    return [ref.at[pl.ds(g * 3 * PER, 3 * PER)] for g in groups]


def clear(scratch):
    for ref in scratch:
        ref[...] = jnp.zeros(ref.shape, F32)


def first_kernel(height, rhs_ref, up_ref, down_ref, left_ref, right_ref, left_ends, right_ends, cm, cs,
                 u0_all, u1_all, u2_all, u3_all, s0_all, s1_all, s2_all, s3_all, totals_out, side, strip_q, sides, sums):
    scratch = (side, strip_q)
    group = pl.program_id(0)
    ext = cm.shape[1]

    @pl.when(group == 0)
    def _():
        clear(scratch)
        clear((sums,))

    groups = [group * PAIR + n for n in range(PAIR)]
    chain = [mine(ref, groups) for ref in (u0_all, u1_all, u2_all, u3_all)]
    strips = [[ref.at[g] for g in groups] for ref in (s0_all, s1_all, s2_all, s3_all)]
    for n, g in enumerate(groups):
        u0, s0 = chain[0][n], strips[0][n]
        for c in range(3):
            join_sides(sides, c, (0, c), (left_ref, right_ref), (left_ends, right_ends), height)
            for i in range(PER):
                k = 3 * (n * PER + i) + c
                join_rows(u0, (3 * i + c,), rhs_ref[k, :, :], up_ref[k * HALO:(k + 1) * HALO, :],
                          down_ref[k * HALO:(k + 1) * HALO, :], height)
            for r in range(0, ext, 8):
                total = jnp.zeros((8, 128), F32)
                for i in range(PER):
                    x = u0[3 * i + c, r:r + 8, :] * cm[19, r:r + 8, :]
                    u0[3 * i + c, r:r + 8, :] = x
                    total = own_columns(x, i, total)
                total = other_columns(sides[0, c, r:r + 8, :], sides[1, c, r:r + 8, :], g % 4, total)
                s0[c, r:r + 8, :] = total * cs[19, r:r + 8, :]
    for j, (first, rows) in enumerate(((TOP - 6, height + 16), (TOP - 5, height + 16), (TOP - 4, height + 8))):
        apply_groups(chain[j], strips[j], chain[j + 1], strips[j + 1], cm, cs, scratch, first, rows // 8)
    for n, g in enumerate(groups):
        vectors = [v[n] for v in chain]
        for i in range(PER):
            rows = [inner(vectors[k // 2], vectors[(k + 1) // 2], i, TOP, TOP, height) for k in range(6)]
            total = None
            for c in range(3):
                for r in range(0, height, 8):
                    t = rhs_ref[3 * (n * PER + i) + c, r:r + 8, :] - vectors[0][3 * i + c, TOP + r:TOP + r + 8, :]
                    t = t * t
                    total = t if total is None else total + t
            rows.append(fold(total))
            for k in range(7):
                sums[k, pl.ds(g * PER + i, 1), :] = rows[k]

    @pl.when(group == pl.num_programs(0) - 1)
    def _():
        add_up(sums, totals_out)


def spread(table, load, i):
    return jnp.broadcast_to(table[pl.ds(load, 1), i:i + 1], (8, 128))


def transposed(keep, square, table):
    square[...] = jnp.zeros((128, 128), F32)
    square[0:32, :] = keep[...]
    table[...] = square[...].T


def second_kernel(height, totals_ref, u0_all, u1_all, u2_all, u3_all, s0_all, s1_all, s2_all, s3_all, cm, cs,
                  w0_all, w1_all, w2_all, w3_all, totals_out, keep_ref, side, strip_q, square, table, t0, t1, t2, sums):
    scratch = (side, strip_q)
    group = pl.program_id(0)

    @pl.when(group == 0)
    def _():
        clear(scratch)
        clear((sums,))
        keep_ref[...] = jnp.zeros(keep_ref.shape, F32)
        middle_scalars(totals_ref, keep_ref)
        transposed(keep_ref, square, table)

    groups = [group * PAIR + n for n in range(PAIR)]
    early = [mine(ref, groups) for ref in (u0_all, u1_all, u2_all, u3_all)]
    chain = [mine(ref, groups) for ref in (w0_all, w1_all, w2_all, w3_all)]
    strips = [[ref.at[g] for g in groups] for ref in (s0_all, s1_all, s2_all, s3_all)]
    chunks = (height + 8) // 8
    window = range(TOP - 4, TOP - 4 + 8 * chunks, 8)
    segment = lanes() // PITCH
    for n, g in enumerate(groups):
        weights = [[spread(table, g * PER + i, j) for j in range(4)] for i in range(PER)]
        for i in range(PER):
            for c in range(3):
                for r in window:
                    x = weights[i][0] * early[0][n][3 * i + c, r:r + 8, :]
                    for j in range(1, 4):
                        x = x + weights[i][j] * early[j][n][3 * i + c, r:r + 8, :]
                    chain[0][n][3 * i + c, r:r + 8, :] = x
        mixed = []
        for j in range(4):
            m = weights[0][j]
            for i in range(1, PER):
                m = jnp.where(segment == i, weights[i][j], m)
            mixed.append(m)
        for c in range(3):
            for r in window:
                x = mixed[0] * strips[0][n][c, r:r + 8, :]
                for j in range(1, 4):
                    x = x + mixed[j] * strips[j][n][c, r:r + 8, :]
                t0[n, c, r:r + 8, :] = x
    late = [[t.at[n] for n in range(PAIR)] for t in (t0, t1, t2)] + [None]
    for j in range(3):
        apply_groups(chain[j], late[j], chain[j + 1], late[j + 1], cm, cs, scratch, TOP - 4, chunks)
    for n, g in enumerate(groups):
        vectors = [v[n] for v in chain]
        for i in range(PER):
            for k in range(6):
                sums[k, pl.ds(g * PER + i, 1), :] = inner(
                    vectors[k // 2], vectors[(k + 1) // 2], i, TOP, TOP, height)

    @pl.when(group == pl.num_programs(0) - 1)
    def _():
        add_up(sums, totals_out)


def last_kernel(height, totals_ref, keep_ref, rhs_ref, u0_all, u1_all, u2_all, w0_all, w1_all, w2_all, w3_all,
                x_ref, r_ref, rows, square, table):
    group = pl.program_id(0)

    @pl.when(group == 0)
    def _():
        rows[...] = jnp.zeros(rows.shape, F32)
        last_scalars(keep_ref, totals_ref, rows)
        transposed(rows, square, table)

    mine = pl.ds(group * 3 * PER, 3 * PER)
    basis = [ref.at[mine] for ref in (u0_all, u1_all, u2_all, w0_all, w1_all, w2_all, w3_all)]
    for i in range(PER):
        f = [spread(table, group * PER + i, j) for j in range(16)]
        for c in range(3):
            k = 3 * i + c
            for r in range(0, height, 8):
                vectors = [ref[k, TOP + r:TOP + r + 8, :] for ref in basis]
                vectors.append(rhs_ref[k, r:r + 8, :] - vectors[0])
                for out, at in ((x_ref, 0), (r_ref, 8)):
                    total = f[at] * vectors[0]
                    for j in range(1, 8):
                        total = total + f[at + j] * vectors[j]
                    out[k, r:r + 8, :] = total


def rows_kernel(*refs):
    low_refs, high_refs, outs = refs[:6], refs[6:12], refs[12:]
    loads = low_refs[0].shape[0]
    for j in range(loads + 18):
        to = slice(j * HALO, (j + 1) * HALO)
        for source, rows, out in ((low_refs, slice(0, HALO), outs[0]), (high_refs, slice(8 - HALO, 8), outs[1])):
            if j < loads:
                out[to, :] = source[0][j, rows, :]
            else:
                out[to, :] = field(source[1:], j - loads, rows)


def cut(get, rows, quarters, right_ref, left_ref):
    lane = lanes() % PITCH
    segment = lanes() // PITCH
    for c in range(3):
        for r in rows:
            right = jnp.zeros((8, 128), F32)
            left = right
            for q in range(quarters):
                for i in range(PER):
                    spot = (segment == i) & (lane >= 8 * q) & (lane < 8 * q + HALO)
                    x = get(q, i, c, r)
                    right = jnp.where(spot, pltpu.roll(x, (PITCH * i + 8 * q + HALO) % 128, 1), right)
                    left = jnp.where(spot, pltpu.roll(x, (PITCH * i + 8 * q) % 128, 1), left)
            right_ref[0, c, r:r + 8, :] = right
            left_ref[0, c, r:r + 8, :] = left


def each_group(merged, load_rows, raw_rows, rows, outs):
    group = pl.program_id(0)

    @pl.when(group < merged)
    def _():
        cut(lambda q, i, c, r: load_rows(3 * (PER * q + i) + c, r), rows, 4, *outs)

    for p in (0, 4):
        @pl.when(group == merged + p // 4)
        def _():
            cut(lambda q, i, c, r: raw_rows(3 * (p + q) + c, r), rows, min(4, 6 - p), *outs)


def columns_kernel(merged, height, data_ref, *refs):
    each_group(
        merged, lambda k, r: data_ref[k, r:r + 8, :], lambda k, r: field(refs[:5], k, slice(r, r + 8)),
        range(0, height, 8), refs[5:],
    )


def ends_kernel(merged, loads, down_ref, up_ref, right_ref, left_ref):
    stop = down_ref.shape[0]

    def rows_at(k, r):
        ref = (down_ref, up_ref)[r // 8]
        if k * HALO + 8 > stop:
            return pltpu.roll(ref[stop - 8:stop, :], HALO, 0)
        return ref[k * HALO:k * HALO + 8, :]

    for h in range(merged):
        cut(lambda q, i, c, r: rows_at(3 * (PER * (4 * h + q) + i) + c, r), (0, 8), 4,
            right_ref.at[h:h + 1], left_ref.at[h:h + 1])
    for p in (0, 4):
        h = merged + p // 4
        cut(lambda q, i, c, r: rows_at(3 * (loads + p + q) + c, r), (0, 8), min(4, 6 - p),
            right_ref.at[h:h + 1], left_ref.at[h:h + 1])


def moved(block, axis, distance):
    n = lax.axis_size(axis)
    return lax.ppermute(block, axis, [(i, i + distance) for i in range(n) if 0 <= i + distance < n])


def gathered(x):
    n = lax.axis_size("gx") * lax.axis_size("gy")
    return lax.all_to_all(jnp.broadcast_to(x[None], (n,) + x.shape), ("gx", "gy"), 0, 0, tiled=True)


def params(limit=8):
    return pltpu.CompilerParams(vmem_limit_bytes=limit * 2**20)


def shape(*dims):
    return jax.ShapeDtypeStruct(dims, F32)


def body(rhs, stiffness, coupling, edges, flip, pinned):
    loads, _, height, width = rhs.shape
    ext = height + 24
    groups = loads // PER
    merged = (groups + 3) // 4
    main = rhs.reshape(loads * 3, height, width)
    raw = (stiffness, coupling, edges, flip, pinned)
    fields = loads * 3 + 18

    def end_block(x, at):
        block = x.shape[:-2] + (8, width)
        lead = (0,) * (x.ndim - 2)
        return pl.BlockSpec(block, lambda g: lead + (at, 0))

    low, high = pl.pallas_call(
        rows_kernel,
        grid=(1,),
        in_specs=[end_block(x, at) for at in (0, height // 8 - 1) for x in (main,) + raw],
        out_specs=[pl.BlockSpec((fields * HALO, width), lambda g: (0, 0))] * 2,
        out_shape=[shape(fields * HALO, width)] * 2,
        compiler_params=params(60),
    )(main, *raw, main, *raw)
    up = moved(low, "gx", -1)
    down = moved(high, "gx", 1)

    count = merged + 2
    wide = 4 * 3 * PER

    def sent(right, left):
        return moved(right, "gy", 1), moved(left, "gy", -1)

    resident = pl.BlockSpec(memory_space=pltpu.VMEM)
    part = pl.BlockSpec((1, 3, height, width), lambda h: (h, 0, 0, 0))
    from_left, from_right = sent(*pl.pallas_call(
        functools.partial(columns_kernel, merged, height),
        grid=(count,),
        in_specs=[pl.BlockSpec((wide, height, width), lambda h: (jnp.minimum(h, merged - 1), 0, 0))] + [resident] * 5,
        out_specs=[part] * 2,
        out_shape=[shape(count, 3, height, width)] * 2,
        compiler_params=params(),
    )(main, *raw))
    left_ends, right_ends = sent(*pl.pallas_call(
        functools.partial(ends_kernel, merged, loads),
        out_shape=[shape(count, 3, 16, width)] * 2,
        compiler_params=params(),
    )(down, up))
    cm, cs = pl.pallas_call(
        functools.partial(prepare_kernel, loads, merged),
        out_shape=[shape(NCOEF, ext, width), shape(NCOEF, ext, width)],
        scratch_shapes=[pltpu.VMEM((6, 3, ext, width), F32)] * 2 + [pltpu.VMEM((2, 3, ext, width), F32)],
        compiler_params=params(),
    )(*raw, up, down, from_left, from_right, left_ends, right_ends)

    own_tile = pl.BlockSpec((3 * PER, height, width), lambda g: (g, 0, 0))
    own_tiles = pl.BlockSpec((3 * PER * PAIR, height, width), lambda g: (g, 0, 0))
    line = pl.BlockSpec((3 * PER * PAIR * HALO, width), lambda g: (g, 0))
    quarter = pl.BlockSpec((1, 3, height, width), lambda g: (PAIR * g // 4, 0, 0, 0))
    corner = pl.BlockSpec((1, 3, 16, width), lambda g: (PAIR * g // 4, 0, 0, 0))
    part = pl.BlockSpec((8, 128), lambda g: (0, 0))
    tiles = pltpu.VMEM((loads * 3, ext, width), F32)
    strips = pltpu.VMEM((groups, 3, ext, width), F32)
    own_shape = shape(loads * 3, height, width)
    sums_shape = shape(8, 128)
    sums_buffer = pltpu.VMEM((7, 128, 128), F32)
    small = [pltpu.VMEM((PAIR, 3, ext, width), F32)] * 2
    u0, u1, u2, u3, s0, s1, s2, s3, sums = pl.pallas_call(
        functools.partial(first_kernel, height),
        grid=(groups // PAIR,),
        in_specs=[own_tiles, line, line, quarter, quarter] + [corner] * 2 + [resident] * 2,
        out_specs=[resident] * 8 + [part],
        out_shape=[tiles] * 4 + [strips] * 4 + [sums_shape],
        scratch_shapes=small + [pltpu.VMEM((2, 3, ext, width), F32), sums_buffer],
        compiler_params=params(),
    )(main, up, down, from_left, from_right, left_ends, right_ends, cm, cs)
    totals = gathered(sums)
    fixed = resident
    kept = pl.BlockSpec((32, 128), lambda g: (0, 0))
    w0, w1, w2, w3, sums, keep = pl.pallas_call(
        functools.partial(second_kernel, height),
        grid=(groups // PAIR,),
        in_specs=[fixed] + [resident] * 10,
        out_specs=[resident] * 4 + [part, kept],
        out_shape=[tiles] * 4 + [sums_shape, shape(32, 128)],
        scratch_shapes=small + [pltpu.VMEM((128, 128), F32)] * 2 + [pltpu.VMEM((PAIR, 3, ext, width), F32)] * 3
        + [sums_buffer],
        compiler_params=params(),
    )(totals, u0, u1, u2, u3, s0, s1, s2, s3, cm, cs)
    totals = gathered(sums)
    x, r = pl.pallas_call(
        functools.partial(last_kernel, height),
        grid=(groups,),
        in_specs=[fixed, kept, own_tile] + [resident] * 7,
        out_specs=[own_tile] * 2,
        out_shape=[own_shape] * 2,
        scratch_shapes=[pltpu.VMEM((32, 128), F32), pltpu.VMEM((128, 128), F32), pltpu.VMEM((128, 128), F32)],
        compiler_params=params(),
    )(totals, keep, main, u0, u1, u2, w0, w1, w2, w3)
    return x.reshape(rhs.shape), r.reshape(rhs.shape)


def solution(mesh):
    placed = (
        P(None, None, "gx", "gy"),
        P(None, "gx", "gy"),
        P(None, "gx", "gy"),
        P(None, "gx", "gy"),
        P("gx", "gy"),
        P("gx", "gy"),
    )
    return jax.shard_map(
        body,
        mesh=mesh,
        in_specs=placed,
        out_specs=(P(None, None, "gx", "gy"), P(None, None, "gx", "gy")),
        check_vma=False,
    )
```

```python
import functools
import jax
import jax.numpy as jnp
from jax import lax
from jax.experimental import pallas as pl
from jax.experimental.pallas import tpu as pltpu
from jax.sharding import PartitionSpec as P

DAMP = 0.2
HALO = 6
TOP = 12
PITCH = 32
PER = 4
NCOEF = 20
PAIR = 2
F32 = jnp.float32


def two_sum(a, b):
    s = a + b
    t = s - a
    return s, (a - (s - t)) + (b - t)


def quick(a, b):
    s = a + b
    return s, b - (s - a)


def halves(a):
    t = 4097.0 * a
    high = t - (t - a)
    return high, a - high


def two_mul(a, b):
    p = a * b
    ah, al = halves(a)
    bh, bl = halves(b)
    return p, ((ah * bh - p) + ah * bl + al * bh) + al * bl


def dd_add(x, y):
    s, e = two_sum(x[0], y[0])
    return quick(s, e + (x[1] + y[1]))


def dd_neg(x):
    return -x[0], -x[1]


def dd_sub(x, y):
    return dd_add(x, dd_neg(y))


def dd_mul(x, y):
    p, e = two_mul(x[0], y[0])
    return quick(p, e + (x[0] * y[1] + x[1] * y[0]))


def dd_div(x, y):
    q = x[0] / y[0]
    p, e = two_mul(q, y[0])
    rest = ((x[0] - p) - e) + (x[1] - q * y[1])
    return quick(q, rest / y[0])


def lift(x):
    return x, jnp.zeros_like(x)


def dd_fma(x, a, y):
    return dd_sub(x, dd_mul(a, y))


def first_block(m):
    one = [dd_div(m[1], m[0])]
    a0 = one[0]
    s1 = {l: dd_fma(m[l + 1], a0, m[l]) for l in range(1, 5)}
    q1 = dd_div(s1[2], s1[1])
    a1 = dd_sub(q1, a0)
    b1 = dd_div(s1[1], m[0])
    s2 = {l: dd_fma(dd_fma(s1[l + 1], a1, s1[l]), b1, m[l]) for l in range(2, 4)}
    a2 = dd_sub(dd_div(s2[3], s2[2]), q1)
    b2 = dd_div(s2[2], s1[1])
    return (a0, a1, a2), (b1, b2), s2[2]


def second_block(nu, a, b, b3):
    a0, a1, a2 = a
    b1, b2 = b
    t2 = {1: nu[0]}
    t2[2] = dd_add(nu[1], dd_mul(a2, t2[1]))
    t12 = nu[0]
    t2[3] = dd_add(dd_add(nu[2], dd_mul(a2, t2[2])), dd_mul(b2, t12))
    t13 = dd_add(t2[2], dd_mul(a1, t12))
    t2[4] = dd_add(dd_add(nu[3], dd_mul(a2, t2[3])), dd_mul(b2, t13))
    a3 = dd_div(nu[1], nu[0])
    t4 = {j: dd_fma(dd_fma(nu[j + 1], a3, nu[j]), b3, t2[j]) for j in range(1, 5)}
    b4 = dd_div(t4[1], nu[0])
    q4 = dd_div(t4[2], t4[1])
    a4 = dd_sub(q4, a3)
    t5 = {j: dd_fma(dd_fma(t4[j + 1], a4, t4[j]), b4, nu[j]) for j in (2, 3)}
    b5 = dd_div(t5[2], t4[1])
    a5 = dd_sub(dd_div(t5[3], t5[2]), q4)
    return (a3, a4, a5), (b4, b5)


def steps_of(a, b, before):
    alphas, sigmas = [], []
    for ak, bk in zip(a, b):
        if before is None:
            alpha = 1.0 / (ak + DAMP)
            sigma = jnp.zeros_like(alpha)
        else:
            ratio = bk * before
            alpha = 1.0 / (ak + DAMP - ratio)
            sigma = alpha * ratio
        alphas.append(alpha)
        sigmas.append(sigma)
        before = alpha
    return alphas, sigmas


def early_residuals(alphas, sigmas):
    one = jnp.ones_like(alphas[0])
    zero = jnp.zeros_like(one)
    polys = [[one, zero, zero, zero]]
    pins = [one]
    for k in range(3):
        now = polys[-1]
        old = polys[-2] if k else [zero] * 4
        lead = 1.0 + sigmas[k] - DAMP * alphas[k]
        polys.append([
            lead * now[i] - (alphas[k] * now[i - 1] if i else zero) - sigmas[k] * old[i]
            for i in range(4)
        ])
        pins.append((1.0 + sigmas[k] - alphas[k]) * pins[-1] - (sigmas[k] * pins[-2] if k else zero))
    return polys, pins


PIN = 1.0 - DAMP


def with_pins(sums, weight):
    out = []
    factor = 1.0
    for k in range(6):
        out.append(dd_add(sums[k], dd_mul(weight, lift(jnp.full_like(weight[0], factor)))))
        factor *= PIN
    return out


def row(ref, i):
    return ref[i:i + 1, :]


def pair_sums(parts_ref):
    def step(d, total):
        high, low = total
        high, error = two_sum(high, parts_ref[d])
        return high, low + error
    zero = jnp.zeros(parts_ref.shape[1:], F32)
    high, low = lax.fori_loop(1, parts_ref.shape[0], step, (parts_ref[0], zero))
    return [quick(high[i:i + 1, :], low[i:i + 1, :]) for i in range(7)]


def middle_scalars(parts_ref, keep_ref):
    sums = pair_sums(parts_ref)
    m = with_pins(sums, sums[6])
    a, b, top = first_block(m)
    alphas, sigmas = steps_of([x[0] for x in a], [None] + [x[0] for x in b], None)
    polys, pins = early_residuals(alphas, sigmas)
    lead = alphas[0] * alphas[1] * alphas[2]
    values = list(polys[3]) + [pins[3], pins[2]]
    values += [x for pair in a + b for x in pair]
    values += [top[0], sums[6][0]] + alphas + sigmas + [lead]
    for i, value in enumerate(values):
        keep_ref[i:i + 1, :] = value


def last_scalars(keep_ref, parts_ref, out_ref):
    kept = [row(keep_ref, i) for i in range(25)]
    pins = [kept[5], kept[4]]
    a = [(kept[6 + 2 * i], kept[7 + 2 * i]) for i in range(3)]
    b = [(kept[12 + 2 * i], kept[13 + 2 * i]) for i in range(2)]
    top, weight = kept[16], kept[17]
    alphas, sigmas = kept[18:21], kept[21:24]
    lead = kept[24]
    nu = with_pins(pair_sums(parts_ref), lift(weight * kept[4] * kept[4]))
    b3 = dd_div(nu[0], dd_mul(lift(top), dd_mul(lift(lead), lift(lead))))
    a_late, b_late = second_block(nu, a, b, b3)
    more, more_sigmas = steps_of(
        [x[0] for x in a_late], [b3[0]] + [x[0] for x in b_late], alphas[2]
    )
    alphas = alphas + more
    sigmas = sigmas + more_sigmas
    one = jnp.ones_like(top)
    zero = jnp.zeros_like(top)

    def unit(i):
        return [one if j == i else zero for j in range(7)]

    def scale(f, v):
        return [f * x for x in v]

    def plus(*vs):
        total = list(vs[0])
        for v in vs[1:]:
            total = [p + q for p, q in zip(total, v)]
        return total

    residuals = [unit(0), unit(1), unit(2), unit(3)]

    def times_h(v):
        out = [zero] * 7
        for k in range(3):
            image = scale((1.0 + sigmas[k]) / alphas[k] - DAMP, unit(k))
            image[k + 1] = image[k + 1] - 1.0 / alphas[k]
            if k:
                image[k - 1] = image[k - 1] - sigmas[k] / alphas[k]
            out = plus(out, scale(v[k], image))
        for k in range(3, 6):
            out[k + 1] = out[k + 1] + v[k]
        return out

    for k in range(3, 6):
        now, old = residuals[k], residuals[k - 1]
        residuals.append(plus(
            scale(1.0 + sigmas[k] - DAMP * alphas[k], now),
            scale(-alphas[k], times_h(now)),
            scale(-sigmas[k], old),
        ))
        pins.append((1.0 + sigmas[k] - alphas[k]) * pins[-1] - sigmas[k] * pins[-2])
    answers = [[zero] * 7, scale(alphas[0], unit(0))]
    for k in range(1, 6):
        answers.append(plus(
            scale(1.0 + sigmas[k], answers[k]), scale(alphas[k], residuals[k]), scale(-sigmas[k], answers[k - 1])
        ))
    polys, early = early_residuals(alphas[:3], sigmas[:3])
    pins_all = early[:3] + pins[1:]
    pin_answers = [zero, alphas[0]]
    for k in range(1, 6):
        pin_answers.append(
            (1.0 + sigmas[k]) * pin_answers[k] + alphas[k] * pins_all[k] - sigmas[k] * pin_answers[k - 1]
        )
    rows = []
    for v, pin in ((answers[6], pin_answers[6]), (residuals[6], pins_all[6])):
        for i in range(3):
            rows.append(v[0] * polys[0][i] + v[1] * polys[1][i] + v[2] * polys[2][i])
        rows += v[3:] + [pin]
    for i, value in enumerate(rows):
        out_ref[i:i + 1, :] = value


def lanes(rows=8):
    return lax.broadcasted_iota(jnp.int32, (rows, 128), 1)


def field(refs, i, rows):
    stiffness, coupling, edges, flip, pinned = refs
    if i < 2:
        return stiffness[i, rows, :]
    if i < 4:
        return coupling[i - 2, rows, :]
    if i < 16:
        return edges[i - 4, rows, :]
    if i == 16:
        return flip[rows, :].astype(F32)
    return (1 - pinned[rows, :]).astype(F32)


def join_rows(dst, lead, own, up, down, height):
    ext = dst.shape[-2]
    dst[lead + (slice(0, 8),)] = jnp.zeros((8, 128), F32)
    dst[lead + (slice(ext - 8, ext),)] = jnp.zeros((8, 128), F32)
    dst[lead + (slice(TOP, TOP + height),)] = own
    dst[lead + (slice(TOP - HALO, TOP),)] = down
    dst[lead + (slice(TOP + height, TOP + height + HALO),)] = up


def own_columns(x, i, kept):
    lane = lanes() % PITCH
    here = lanes() // PITCH == i
    kept = jnp.where(here & (lane >= 6) & (lane < 12), pltpu.roll(x, PITCH * i + 6, 1), kept)
    return jnp.where(here & (lane >= 16) & (lane < 21), pltpu.roll(x, (PITCH * i + 16 - 123) % 128, 1), kept)


def other_columns(left, right, q, kept):
    lane = lanes() % PITCH
    kept = jnp.where(lane < HALO, pltpu.roll(left, (128 - 8 * q) % 128, 1), kept)
    return jnp.where(
        (lane >= 21) & (lane < 21 + HALO), pltpu.roll(right, (128 + 21 - 8 * q) % 128, 1), kept)


def join_sides(sides, column, lead, merged, corners, height):
    for n in range(2):
        join_rows(sides, (n, column), merged[n][lead + (slice(None),)], corners[n][lead + (slice(8, 8 + HALO),)],
                  corners[n][lead + (slice(0, HALO),)], height)


def prepare_kernel(loads, merged, stiffness, coupling, edges, flip, pinned, up_ref, down_ref, left_ref, right_ref, left_ends, right_ends,
                   main_out, strip_out, wide, strip, sides):
    refs = (stiffness, coupling, edges, flip, pinned)
    height = flip.shape[0]
    ext = wide.shape[2]
    for p in range(6):
        for c in range(3):
            k = 3 * (loads + p) + c
            join_rows(wide, (p, c), field(refs, 3 * p + c, slice(0, height)), up_ref[k * HALO:(k + 1) * HALO, :],
                      down_ref[k * HALO:(k + 1) * HALO, :], height)
            join_sides(sides, c, (merged + p // 4, c), (left_ref, right_ref), (left_ends, right_ends), height)
            for r in range(0, ext, 8):
                x = wide[p, c, r:r + 8, :]
                total = jnp.zeros((8, 128), F32)
                for i in range(PER):
                    total = own_columns(x, i, total)
                strip[p, c, r:r + 8, :] = other_columns(
                    sides[0, c, r:r + 8, :], sides[1, c, r:r + 8, :], p % 4, total)
    lane = lax.broadcasted_iota(jnp.int32, (ext, 128), 1)
    line = lax.broadcasted_iota(jnp.int32, (ext, 128), 0)
    near = None
    for which, (src, dst) in enumerate(((strip, strip_out), (wide, main_out))):
        def raw(i):
            return src[i // 3, i % 3]
        flipped = raw(16) > 0.5
        zero = jnp.zeros((ext, 128), F32)
        k1, k2 = raw(0), raw(1)
        root1, root2 = jnp.sqrt(raw(2)), jnp.sqrt(raw(3))
        other = jnp.where(flipped, zero, k2)
        left = pltpu.roll(other, 1, 1)
        if which == 1:
            left = jnp.where(lane == 0, near, left)
        else:
            near = pltpu.roll(other, 128 - (HALO - 1), 1)
        below = jnp.where(line == 0, zero, pltpu.roll(other, 1, 0))
        dst[0] = k1 + left
        dst[1] = jnp.where(flipped, k2, k1) + below
        dst[2] = jnp.where(flipped, k1 + k2, zero)
        for c in range(3):
            dst[3 + c] = root1 * raw(4 + c)
            dst[6 + c] = root1 * raw(7 + c)
            one = root2 * raw(10 + c)
            two = root2 * raw(13 + c)
            dst[9 + c] = jnp.where(flipped, zero, two)
            dst[12 + c] = jnp.where(flipped, two, one)
            dst[15 + c] = jnp.where(flipped, one, -(one + two))
        dst[18] = raw(16)
        dst[19] = raw(17)


def dot3(p, q):
    return p[0] * q[0] + p[1] * q[1] + p[2] * q[2]


def tile_step(tiles, coef, first, chunks):
    stop = first + 8 * chunks
    for r in list(range(first, stop, 8)) + [stop - 7]:
        for side, get, beside, _, _, _ in tiles:
            for c in range(3):
                side[c, r:r + 8, :] = beside(c, r, get(c, r))
    top = lax.broadcasted_iota(jnp.int32, (8, 128), 0) == 0
    before = [None] * len(tiles)
    for r in range(first, stop, 8):
        def co(i):
            return coef[i, r:r + 8, :]
        flipped = co(18) > 0.5
        g1 = [co(3 + c) for c in range(3)]
        g2 = [co(6 + c) for c in range(3)]
        hb = [co(9 + c) for c in range(3)]
        hc = [co(12 + c) for c in range(3)]
        hd = [co(15 + c) for c in range(3)]
        wv, wh, wd, free = co(0), co(1), co(2), co(19)
        forces = []
        for side, get, _, _, _, _ in tiles:
            base = [get(c, r) for c in range(3)]
            eb = [get(c, r + 1) - base[c] for c in range(3)]
            ec = [side[c, r:r + 8, :] - base[c] for c in range(3)]
            ed = [side[c, r + 1:r + 9, :] - base[c] for c in range(3)]
            ex = [jnp.where(flipped, ed[c], ec[c]) for c in range(3)]
            s1 = dot3(g1, eb) + dot3(g2, ex)
            s2 = dot3(hb, eb) + dot3(hc, ec) + dot3(hd, ed)
            zero = jnp.zeros_like(s1)
            s1c = jnp.where(flipped, zero, s1)
            s1d = jnp.where(flipped, s1, zero)
            forces.append([(
                wv * eb[c] + s1 * g1[c] + s2 * hb[c],
                wh * ec[c] + s1c * g2[c] + s2 * hc[c],
                wd * ed[c] + s1d * g2[c] + s2 * hd[c],
            ) for c in range(3)])
        for n, (_, _, _, spill, put, put_spill) in enumerate(tiles):
            rolled = []
            for c in range(3):
                fb, fc, fd = forces[n][c]
                down_b, down_d = pltpu.roll(fb, 1, 0), pltpu.roll(fd, 1, 0)
                rolled.append((down_b, down_d))
                if before[n] is not None:
                    down_b = jnp.where(top, before[n][c][0], down_b)
                    down_d = jnp.where(top, before[n][c][1], down_d)
                own = down_b - (fb + fc + fd)
                q = fc + down_d
                if put_spill is not None:
                    put_spill(c, r, q)
                put(c, r, free * (own + spill(c, r, q)))
            before[n] = rolled


def apply_groups(src_mains, src_strips, dst_mains, dst_strips, coef_main, coef_strip, scratch, first, chunks):
    side, strip_q = scratch
    lane = lanes()

    def strip_tile(n):
        def put(c, r, x):
            if dst_strips is not None:
                dst_strips[n][c, r:r + 8, :] = x

        def put_q(c, r, x):
            strip_q[n, c, r:r + 8, :] = x

        return (
            side.at[n],
            lambda c, r: src_strips[n][c, r:r + 8, :],
            lambda c, r, x: pltpu.roll(x, 127, 1),
            lambda c, r, x: pltpu.roll(x, 1, 1),
            put,
            put_q,
        )

    tile_step([strip_tile(n) for n in range(PAIR)], coef_strip, first, chunks)

    def tile(n, i, slot):
        base = 3 * i
        to_last = (127 - (PITCH * i + 21)) % 128
        to_first = (128 - (PITCH * i + HALO - 1)) % 128

        def get(c, r):
            return src_mains[n][base + c, r:r + 8, :]

        def beside(c, r, x):
            beyond = pltpu.roll(src_strips[n][c, r:r + 8, :], to_last, 1)
            return jnp.where(lane == 127, beyond, pltpu.roll(x, 127, 1))

        def spill(c, r, x):
            beyond = pltpu.roll(strip_q[n, c, r:r + 8, :], to_first, 1)
            return jnp.where(lane == 0, beyond, pltpu.roll(x, 1, 1))

        def put(c, r, x):
            dst_mains[n][base + c, r:r + 8, :] = x

        return side.at[slot], get, beside, spill, put, None

    for n in range(PAIR):
        for i in range(0, PER, PAIR):
            tile_step([tile(n, i + j, j) for j in range(PAIR)], coef_main, first, chunks)


def add_up(sums, totals_ref):
    totals_ref[...] = jnp.zeros(totals_ref.shape, F32)
    for k in range(7):
        totals_ref[k:k + 1, :] = jnp.sum(sums[k].T, axis=0, keepdims=True)


def fold(x):
    return jnp.sum(x, axis=0, keepdims=True)


def inner(p_ref, q_ref, i, p_at, q_at, height):
    total = None
    for c in range(3):
        for r in range(0, height, 8):
            t = p_ref[3 * i + c, p_at + r:p_at + r + 8, :] * q_ref[3 * i + c, q_at + r:q_at + r + 8, :]
            total = t if total is None else total + t
    return fold(total)


def mine(ref, groups):
    return [ref.at[pl.ds(g * 3 * PER, 3 * PER)] for g in groups]


def clear(scratch):
    for ref in scratch:
        ref[...] = jnp.zeros(ref.shape, F32)


def first_kernel(height, rhs_ref, up_ref, down_ref, left_ref, right_ref, left_ends, right_ends, cm, cs,
                 u0_all, u1_all, u2_all, u3_all, s0_all, s1_all, s2_all, s3_all, totals_out, side, strip_q, sides, sums):
    scratch = (side, strip_q)
    group = pl.program_id(0)
    ext = cm.shape[1]

    @pl.when(group == 0)
    def _():
        clear(scratch)
        clear((sums,))

    groups = [group * PAIR + n for n in range(PAIR)]
    chain = [mine(ref, groups) for ref in (u0_all, u1_all, u2_all, u3_all)]
    strips = [[ref.at[g] for g in groups] for ref in (s0_all, s1_all, s2_all, s3_all)]
    for n, g in enumerate(groups):
        u0, s0 = chain[0][n], strips[0][n]
        for c in range(3):
            join_sides(sides, c, (0, c), (left_ref, right_ref), (left_ends, right_ends), height)
            for i in range(PER):
                k = 3 * (n * PER + i) + c
                join_rows(u0, (3 * i + c,), rhs_ref[k, :, :], up_ref[k * HALO:(k + 1) * HALO, :],
                          down_ref[k * HALO:(k + 1) * HALO, :], height)
            for r in range(0, ext, 8):
                total = jnp.zeros((8, 128), F32)
                for i in range(PER):
                    x = u0[3 * i + c, r:r + 8, :] * cm[19, r:r + 8, :]
                    u0[3 * i + c, r:r + 8, :] = x
                    total = own_columns(x, i, total)
                total = other_columns(sides[0, c, r:r + 8, :], sides[1, c, r:r + 8, :], g % 4, total)
                s0[c, r:r + 8, :] = total * cs[19, r:r + 8, :]
    for j, (first, rows) in enumerate(((TOP - 6, height + 16), (TOP - 5, height + 16), (TOP - 4, height + 8))):
        apply_groups(chain[j], strips[j], chain[j + 1], strips[j + 1], cm, cs, scratch, first, rows // 8)
    for n, g in enumerate(groups):
        vectors = [v[n] for v in chain]
        for i in range(PER):
            rows = [inner(vectors[k // 2], vectors[(k + 1) // 2], i, TOP, TOP, height) for k in range(6)]
            total = None
            for c in range(3):
                for r in range(0, height, 8):
                    t = rhs_ref[3 * (n * PER + i) + c, r:r + 8, :] - vectors[0][3 * i + c, TOP + r:TOP + r + 8, :]
                    t = t * t
                    total = t if total is None else total + t
            rows.append(fold(total))
            for k in range(7):
                sums[k, pl.ds(g * PER + i, 1), :] = rows[k]

    @pl.when(group == pl.num_programs(0) - 1)
    def _():
        add_up(sums, totals_out)


def spread(table, load, i):
    return jnp.broadcast_to(table[pl.ds(load, 1), i:i + 1], (8, 128))


def transposed(keep, square, table):
    square[...] = jnp.zeros((128, 128), F32)
    square[0:32, :] = keep[...]
    table[...] = square[...].T


def second_kernel(height, totals_ref, u0_all, u1_all, u2_all, u3_all, s0_all, s1_all, s2_all, s3_all, cm, cs,
                  w0_all, w1_all, w2_all, w3_all, totals_out, keep_ref, side, strip_q, square, table, t0, t1, t2, sums):
    scratch = (side, strip_q)
    group = pl.program_id(0)

    @pl.when(group == 0)
    def _():
        clear(scratch)
        clear((sums,))
        keep_ref[...] = jnp.zeros(keep_ref.shape, F32)
        middle_scalars(totals_ref, keep_ref)
        transposed(keep_ref, square, table)

    groups = [group * PAIR + n for n in range(PAIR)]
    early = [mine(ref, groups) for ref in (u0_all, u1_all, u2_all, u3_all)]
    chain = [mine(ref, groups) for ref in (w0_all, w1_all, w2_all, w3_all)]
    strips = [[ref.at[g] for g in groups] for ref in (s0_all, s1_all, s2_all, s3_all)]
    chunks = (height + 8) // 8
    window = range(TOP - 4, TOP - 4 + 8 * chunks, 8)
    segment = lanes() // PITCH
    for n, g in enumerate(groups):
        weights = [[spread(table, g * PER + i, j) for j in range(4)] for i in range(PER)]
        for i in range(PER):
            for c in range(3):
                for r in window:
                    x = weights[i][0] * early[0][n][3 * i + c, r:r + 8, :]
                    for j in range(1, 4):
                        x = x + weights[i][j] * early[j][n][3 * i + c, r:r + 8, :]
                    chain[0][n][3 * i + c, r:r + 8, :] = x
        mixed = []
        for j in range(4):
            m = weights[0][j]
            for i in range(1, PER):
                m = jnp.where(segment == i, weights[i][j], m)
            mixed.append(m)
        for c in range(3):
            for r in window:
                x = mixed[0] * strips[0][n][c, r:r + 8, :]
                for j in range(1, 4):
                    x = x + mixed[j] * strips[j][n][c, r:r + 8, :]
                t0[n, c, r:r + 8, :] = x
    late = [[t.at[n] for n in range(PAIR)] for t in (t0, t1, t2)] + [None]
    for j in range(3):
        apply_groups(chain[j], late[j], chain[j + 1], late[j + 1], cm, cs, scratch, TOP - 4, chunks)
    for n, g in enumerate(groups):
        vectors = [v[n] for v in chain]
        for i in range(PER):
            for k in range(6):
                sums[k, pl.ds(g * PER + i, 1), :] = inner(
                    vectors[k // 2], vectors[(k + 1) // 2], i, TOP, TOP, height)

    @pl.when(group == pl.num_programs(0) - 1)
    def _():
        add_up(sums, totals_out)


def last_kernel(height, totals_ref, keep_ref, rhs_ref, u0_all, u1_all, u2_all, w0_all, w1_all, w2_all, w3_all,
                x_ref, r_ref, rows, square, table):
    group = pl.program_id(0)

    @pl.when(group == 0)
    def _():
        rows[...] = jnp.zeros(rows.shape, F32)
        last_scalars(keep_ref, totals_ref, rows)
        transposed(rows, square, table)

    count = rhs_ref.shape[0] // 3
    mine = pl.ds(group * 3 * count, 3 * count)
    basis = [ref.at[mine] for ref in (u0_all, u1_all, u2_all, w0_all, w1_all, w2_all, w3_all)]
    for i in range(count):
        f = [spread(table, group * count + i, j) for j in range(16)]
        for c in range(3):
            k = 3 * i + c
            for r in range(0, height, 8):
                vectors = [ref[k, TOP + r:TOP + r + 8, :] for ref in basis]
                vectors.append(rhs_ref[k, r:r + 8, :] - vectors[0])
                for out, at in ((x_ref, 0), (r_ref, 8)):
                    total = f[at] * vectors[0]
                    for j in range(1, 8):
                        total = total + f[at + j] * vectors[j]
                    out[k, r:r + 8, :] = total


def rows_kernel(*refs):
    low_refs, high_refs, outs = refs[:6], refs[6:12], refs[12:]
    loads = low_refs[0].shape[0]
    for j in range(loads + 18):
        to = slice(j * HALO, (j + 1) * HALO)
        for source, rows, out in ((low_refs, slice(0, HALO), outs[0]), (high_refs, slice(8 - HALO, 8), outs[1])):
            if j < loads:
                out[to, :] = source[0][j, rows, :]
            else:
                out[to, :] = field(source[1:], j - loads, rows)


def cut(get, rows, quarters, right_ref, left_ref):
    lane = lanes() % PITCH
    segment = lanes() // PITCH
    for c in range(3):
        for r in rows:
            right = jnp.zeros((8, 128), F32)
            left = right
            for q in range(quarters):
                for i in range(PER):
                    spot = (segment == i) & (lane >= 8 * q) & (lane < 8 * q + HALO)
                    x = get(q, i, c, r)
                    right = jnp.where(spot, pltpu.roll(x, (PITCH * i + 8 * q + HALO) % 128, 1), right)
                    left = jnp.where(spot, pltpu.roll(x, (PITCH * i + 8 * q) % 128, 1), left)
            right_ref[0, c, r:r + 8, :] = right
            left_ref[0, c, r:r + 8, :] = left


def each_group(merged, load_rows, raw_rows, rows, outs):
    group = pl.program_id(0)

    @pl.when(group < merged)
    def _():
        cut(lambda q, i, c, r: load_rows(3 * (PER * q + i) + c, r), rows, 4, *outs)

    for p in (0, 4):
        @pl.when(group == merged + p // 4)
        def _():
            cut(lambda q, i, c, r: raw_rows(3 * (p + q) + c, r), rows, min(4, 6 - p), *outs)


def columns_kernel(merged, height, data_ref, *refs):
    each_group(
        merged, lambda k, r: data_ref[k, r:r + 8, :], lambda k, r: field(refs[:5], k, slice(r, r + 8)),
        range(0, height, 8), refs[5:],
    )


def ends_kernel(merged, loads, down_ref, up_ref, right_ref, left_ref):
    stop = down_ref.shape[0]

    def rows_at(k, r):
        ref = (down_ref, up_ref)[r // 8]
        if k * HALO + 8 > stop:
            return pltpu.roll(ref[stop - 8:stop, :], HALO, 0)
        return ref[k * HALO:k * HALO + 8, :]

    for h in range(merged):
        cut(lambda q, i, c, r: rows_at(3 * (PER * (4 * h + q) + i) + c, r), (0, 8), 4,
            right_ref.at[h:h + 1], left_ref.at[h:h + 1])
    for p in (0, 4):
        h = merged + p // 4
        cut(lambda q, i, c, r: rows_at(3 * (loads + p + q) + c, r), (0, 8), min(4, 6 - p),
            right_ref.at[h:h + 1], left_ref.at[h:h + 1])


def moved(block, axis, distance):
    n = lax.axis_size(axis)
    return lax.ppermute(block, axis, [(i, i + distance) for i in range(n) if 0 <= i + distance < n])


def gathered(x):
    n = lax.axis_size("gx") * lax.axis_size("gy")
    return lax.all_to_all(jnp.broadcast_to(x[None], (n,) + x.shape), ("gx", "gy"), 0, 0, tiled=True)


def params(limit=8):
    return pltpu.CompilerParams(vmem_limit_bytes=limit * 2**20)


def shape(*dims):
    return jax.ShapeDtypeStruct(dims, F32)


def body(rhs, stiffness, coupling, edges, flip, pinned):
    loads, _, height, width = rhs.shape
    ext = height + 24
    groups = loads // PER
    merged = (groups + 3) // 4
    main = rhs.reshape(loads * 3, height, width)
    raw = (stiffness, coupling, edges, flip, pinned)
    fields = loads * 3 + 18

    def end_block(x, at):
        block = x.shape[:-2] + (8, width)
        lead = (0,) * (x.ndim - 2)
        return pl.BlockSpec(block, lambda g: lead + (at, 0))

    low, high = pl.pallas_call(
        rows_kernel,
        grid=(1,),
        in_specs=[end_block(x, at) for at in (0, height // 8 - 1) for x in (main,) + raw],
        out_specs=[pl.BlockSpec((fields * HALO, width), lambda g: (0, 0))] * 2,
        out_shape=[shape(fields * HALO, width)] * 2,
        compiler_params=params(60),
    )(main, *raw, main, *raw)
    up = moved(low, "gx", -1)
    down = moved(high, "gx", 1)

    count = merged + 2
    wide = 4 * 3 * PER

    def sent(right, left):
        return moved(right, "gy", 1), moved(left, "gy", -1)

    resident = pl.BlockSpec(memory_space=pltpu.VMEM)
    part = pl.BlockSpec((1, 3, height, width), lambda h: (h, 0, 0, 0))
    from_left, from_right = sent(*pl.pallas_call(
        functools.partial(columns_kernel, merged, height),
        grid=(count,),
        in_specs=[pl.BlockSpec((wide, height, width), lambda h: (jnp.minimum(h, merged - 1), 0, 0))] + [resident] * 5,
        out_specs=[part] * 2,
        out_shape=[shape(count, 3, height, width)] * 2,
        compiler_params=params(),
    )(main, *raw))
    left_ends, right_ends = sent(*pl.pallas_call(
        functools.partial(ends_kernel, merged, loads),
        out_shape=[shape(count, 3, 16, width)] * 2,
        compiler_params=params(),
    )(down, up))
    cm, cs = pl.pallas_call(
        functools.partial(prepare_kernel, loads, merged),
        out_shape=[shape(NCOEF, ext, width), shape(NCOEF, ext, width)],
        scratch_shapes=[pltpu.VMEM((6, 3, ext, width), F32)] * 2 + [pltpu.VMEM((2, 3, ext, width), F32)],
        compiler_params=params(),
    )(*raw, up, down, from_left, from_right, left_ends, right_ends)

    own_tiles = pl.BlockSpec((3 * PER * PAIR, height, width), lambda g: (g, 0, 0))
    line = pl.BlockSpec((3 * PER * PAIR * HALO, width), lambda g: (g, 0))
    quarter = pl.BlockSpec((1, 3, height, width), lambda g: (PAIR * g // 4, 0, 0, 0))
    corner = pl.BlockSpec((1, 3, 16, width), lambda g: (PAIR * g // 4, 0, 0, 0))
    part = pl.BlockSpec((8, 128), lambda g: (0, 0))
    tiles = pltpu.VMEM((loads * 3, ext, width), F32)
    strips = pltpu.VMEM((groups, 3, ext, width), F32)
    own_shape = shape(loads * 3, height, width)
    sums_shape = shape(8, 128)
    sums_buffer = pltpu.VMEM((7, 128, 128), F32)
    small = [pltpu.VMEM((PAIR, 3, ext, width), F32)] * 2
    u0, u1, u2, u3, s0, s1, s2, s3, sums = pl.pallas_call(
        functools.partial(first_kernel, height),
        grid=(groups // PAIR,),
        in_specs=[own_tiles, line, line, quarter, quarter] + [corner] * 2 + [resident] * 2,
        out_specs=[resident] * 8 + [part],
        out_shape=[tiles] * 4 + [strips] * 4 + [sums_shape],
        scratch_shapes=small + [pltpu.VMEM((2, 3, ext, width), F32), sums_buffer],
        compiler_params=params(),
    )(main, up, down, from_left, from_right, left_ends, right_ends, cm, cs)
    totals = gathered(sums)
    fixed = resident
    kept = pl.BlockSpec((32, 128), lambda g: (0, 0))
    w0, w1, w2, w3, sums, keep = pl.pallas_call(
        functools.partial(second_kernel, height),
        grid=(groups // PAIR,),
        in_specs=[fixed] + [resident] * 10,
        out_specs=[resident] * 4 + [part, kept],
        out_shape=[tiles] * 4 + [sums_shape, shape(32, 128)],
        scratch_shapes=small + [pltpu.VMEM((128, 128), F32)] * 2 + [pltpu.VMEM((PAIR, 3, ext, width), F32)] * 3
        + [sums_buffer],
        compiler_params=params(),
    )(totals, u0, u1, u2, u3, s0, s1, s2, s3, cm, cs)
    totals = gathered(sums)
    x, r = pl.pallas_call(
        functools.partial(last_kernel, height),
        grid=(groups // PAIR,),
        in_specs=[fixed, kept, own_tiles] + [resident] * 7,
        out_specs=[own_tiles] * 2,
        out_shape=[own_shape] * 2,
        scratch_shapes=[pltpu.VMEM((32, 128), F32), pltpu.VMEM((128, 128), F32), pltpu.VMEM((128, 128), F32)],
        compiler_params=params(),
    )(totals, keep, main, u0, u1, u2, w0, w1, w2, w3)
    return x.reshape(rhs.shape), r.reshape(rhs.shape)


def solution(mesh):
    placed = (
        P(None, None, "gx", "gy"),
        P(None, "gx", "gy"),
        P(None, "gx", "gy"),
        P(None, "gx", "gy"),
        P("gx", "gy"),
        P("gx", "gy"),
    )
    return jax.shard_map(
        body,
        mesh=mesh,
        in_specs=placed,
        out_specs=(P(None, None, "gx", "gy"), P(None, None, "gx", "gy")),
        check_vma=False,
    )
```
